512 devices in a mesh: req: 32 (over z, y_lo), tp: 16 (over x, y_hi, core).
Axes of the slice: x: 4, y: 8 (y_hi: 2, y_lo: 4; y = y_hi * 4 + y_lo), z: 8, core: 2. Of those that a mesh axis runs over, the one named last changes fastest.
Arguments:
- scan_state: float32 [128, 128, 64, 128], P('req', 'tp'), may hold values from -6 to 6
- decay_rate: float32 [128], P('tp'), may hold values from 0.05 to 3
- step_bias: float32 [128], P('tp'), may hold values from -2 to 1
- skip_gain: float32 [128], P('tp'), may hold values from 0.5 to 2
- norm_gain: float32 [128, 64], P('tp'), may hold values from 0.1 to 1.9
- page_pool: bfloat16 [8192, 16, 2048], P(('req', 'tp')), may hold values from -26 to 26
- old_table: int32 [128, 4, 16], P('req', None, 'tp'), may hold values from 0 to 15, as said below
- new_table: int32 [128, 4, 16], P('req', None, 'tp'), may hold values from 0 to 15, as said below
- request_source: int32 [128], replicated, may hold values from 0 to 127, as said below
- head_source: int32 [128], replicated, may hold values from 0 to 127, as said below
- context_lengths: int32 [128], replicated, may hold values from 1 to 1022
- mixer_input: bfloat16 [2, 128, 8192], P(None, 'req', 'tp'), may hold values from -6 to 6
- mixer_gate: bfloat16 [2, 128, 8192], P(None, 'req', 'tp'), may hold values from -6 to 6
- step_raw: float32 [2, 128, 128], P(None, 'req', 'tp'), may hold values from -4 to 4
- state_maps: bfloat16 [2, 128, 2, 1024], P(None, 'req'), may hold values from -4 to 4
- queries: bfloat16 [2, 128, 8192], P(None, 'req'), may hold values from -26 to 26
- new_entries: bfloat16 [2, 128, 2048], P(None, 'req'), may hold values from -26 to 26
Outputs:
- mixer_out: bfloat16 [2, 128, 8192], P(None, 'req', 'tp')
- attention: bfloat16 [2, 128, 8192], P(None, 'req', 'tp')
- final_state: float32 [128, 128, 64, 128], P('req', 'tp')
- final_pool: bfloat16 [8192, 16, 2048], P(('req', 'tp'))
The draws below stay inside these ranges and needn't reach their ends.
Inputs may be any that keep to these rules, and one draw needn't show every extreme that they name: `request_source`: A permutation: new row p belongs to owner p // 4; its old row belongs to that owner or to one next to it along req. Across each boundary between neighbouring owners the same number of requests moves each way, at most 2, and in every draw some boundary carries exactly 2 each way. `head_source`: A permutation: new slot j belongs to tp index j // 8; its old head belongs to that index or to one next to it. Across each boundary the same number of heads moves each way, at most 4, and in every draw some boundary carries exactly 4 each way. `old_table`: for each owner along req and each tp index t, the entries [p, :, t] of the owner's 4 rows form a permutation of its 16 slots. `new_table`: for each owner along req and each tp index t, the entries [p, :, t] of the owner's 4 rows form a permutation of its 16 slots.
All inputs are finite; a program needn't handle non-finite values.
Results may differ from the reference program's by a relative error of at most 0.0055.
Values may be sent and summed in bfloat16 or wider, within the bound.
A program may use at most 64 MiB of HBM per device.

```python
import math
import jax
import jax.numpy as jnp
from jax import lax

H = 128
P_SIZE = 64
N = 128
G = 8
QH = 64
KVH = 8
HD = 128
PAGE = 16
STEPS = 2
RQ_DEV = 4
PGS = 4
MV = 2
HPD = 8
HMV = 4
REQUESTS = 128
PG_DEV = 16
POOL = 8192
CONTEXT = 1024
KVW = 2048
N_REQ = 32
N_TP = 16


def neighbour_source(key, blocks, width, most):
    key_moves, key_force, key_new, key_old = jax.random.split(key, 4)
    moves = jax.random.randint(key_moves, (blocks - 1,), 1, most + 1)
    forced = jax.random.randint(key_force, (), 0, blocks - 1)
    moves = jnp.where(jnp.arange(blocks - 1) == forced, most, moves).astype(jnp.int32)
    padded = jnp.concatenate([jnp.zeros((1,), jnp.int32), moves, jnp.zeros((1,), jnp.int32)])
    place = jnp.arange(blocks * width, dtype=jnp.int32)
    block = place // width
    offset = place % width
    right_count = padded[block + 1]
    left_count = padded[block]
    source = jnp.where(offset >= width - right_count, (block + 1) * width + offset - (width - right_count), place)
    source = jnp.where(offset < left_count, (block - 1) * width + width - left_count + offset, source)
    new_order = jax.vmap(lambda part_key: jax.random.permutation(part_key, width))(jax.random.split(key_new, blocks))
    old_order = jax.vmap(lambda part_key: jax.random.permutation(part_key, width))(jax.random.split(key_old, blocks))
    source = source[block * width + new_order.reshape(-1).astype(jnp.int32)]
    source_block = source // width
    relabel = old_order.astype(jnp.int32)[source_block, source % width]
    return (source_block * width + relabel).astype(jnp.int32)


def slot_table(key):
    perms = jax.vmap(lambda part_key: jax.random.permutation(part_key, PG_DEV))(jax.random.split(key, N_REQ * N_TP))
    table = perms.astype(jnp.int32).reshape(N_REQ, N_TP, RQ_DEV, PGS)
    return jnp.transpose(table, (0, 2, 3, 1)).reshape(REQUESTS, PGS, N_TP)


def entry_rows(key, leading):
    noise = jnp.clip(jax.random.normal(key, leading + (2, KVH, HD), jnp.float32), -3.0, 3.0)
    keys_part = noise[..., 0, :, :]
    both = jnp.stack([keys_part, noise[..., 1, :, :]], axis=-3)
    return both.reshape(leading + (2 * KVH * HD,)).astype(jnp.bfloat16)


def draw_request_source(key, part):
    key = jax.random.fold_in(key, 11)
    return neighbour_source(key, N_REQ, RQ_DEV, MV)


def draw_head_source(key, part):
    key = jax.random.fold_in(key, 12)
    return neighbour_source(key, N_TP, HPD, HMV)


def draw_old_table(key, part):
    key = jax.random.fold_in(key, 13)
    return slot_table(key)


def draw_new_table(key, part):
    key = jax.random.fold_in(key, 14)
    return slot_table(key)


def draw_queries(key, part):
    key = jax.random.fold_in(key, 15)
    noise = jnp.clip(jax.random.normal(key, (STEPS, REQUESTS, KVH, QH // KVH, HD), jnp.float32), -3.0, 3.0)
    values = noise
    return values.reshape(STEPS, REQUESTS, QH * HD).astype(jnp.bfloat16)


def draw_page_pool(key, part):
    key = jax.random.fold_in(key, 16)
    return entry_rows(key, (POOL, PAGE))


def draw_new_entries(key, part):
    key = jax.random.fold_in(key, 17)
    return entry_rows(key, (STEPS, REQUESTS))


def touch_ends(values, key, low, high):
    longest = values.shape.index(max(values.shape))
    spots = []
    for shift in (0, 1):
        where = [jax.random.randint(jax.random.fold_in(key, axis), (), 0, length) for axis, length in enumerate(values.shape)]
        where[longest] = (where[longest] + shift) % values.shape[longest]
        spots.append(tuple(where))
    return values.at[spots[0]].set(low).at[spots[1]].set(high)


def levels(key, extent, cuts, smallest, top_value):
    level = 1.0
    for axis_at, parts in cuts:
        draws = jax.random.uniform(jax.random.fold_in(jax.random.fold_in(key, 6), axis_at), (parts,), jnp.float32, smallest / len(cuts), top_value / len(cuts))
        level = level * jnp.repeat(jnp.exp(draws), extent[axis_at] // parts).reshape((-1,) + (1,) * (len(extent) - 1 - axis_at))
    return level


def centred(stream_key, extent, deviation, bound, cuts=(), held_as=jnp.bfloat16):
    gain = levels(stream_key, extent, cuts, -0.22, 0.18) if cuts else 1.0
    values = jax.random.normal(stream_key, extent, jnp.float32) * deviation * gain
    return jnp.minimum(jnp.maximum(values, -bound), bound).astype(held_as)


def setup_inputs(seed: int = 0) -> dict:
    splits = jax.random.split(jax.random.key(seed), 18)
    scan_state = centred(splits[0], (REQUESTS, H, P_SIZE, N), 1.0, 6.0, ((0, 32), (1, 16)), jnp.float32)
    decay_rate = jnp.clip(jnp.exp(math.log(3.0) - 4.0943445 * jax.random.uniform(splits[1], (H,), jnp.float32) ** levels(splits[1], (H,), ((0, 16),), -0.2, 0.2)), 0.05, 3.0)
    step_bias = jnp.clip(-2.0 + 3.0 * jax.random.uniform(splits[2], (H,), jnp.float32) ** levels(splits[2], (H,), ((0, 16),), -0.2, 0.2), -2.0, 1.0)
    skip_gain = jnp.clip(0.5 + 1.5 * jax.random.uniform(splits[3], (H,), jnp.float32) ** levels(splits[3], (H,), ((0, 16),), -0.2, 0.2), 0.5, 2.0)
    norm_gain = jnp.clip(1.0 + 0.18 * jax.random.normal(splits[4], (H, P_SIZE), jnp.float32), 0.1, 1.9)
    page_pool = draw_page_pool(jax.random.fold_in(splits[17], 71), 0)
    old_table = draw_old_table(jax.random.fold_in(splits[17], 71), 0)
    new_table = draw_new_table(jax.random.fold_in(splits[17], 71), 0)
    request_source = draw_request_source(jax.random.fold_in(splits[17], 71), 0)
    head_source = draw_head_source(jax.random.fold_in(splits[17], 71), 0)
    context_lengths = touch_ends(jax.random.randint(splits[10], (REQUESTS,), 1, CONTEXT - 1), jax.random.fold_in(splits[10], 1), 1, (CONTEXT - 1) - 1).astype(jnp.int32)
    mixer_input = centred(splits[11], (STEPS, REQUESTS, H * P_SIZE), 1.0, 6.0, ((1, 32), (2, 16)))
    mixer_gate = centred(splits[12], (STEPS, REQUESTS, H * P_SIZE), 1.0, 6.0, ((1, 32), (2, 16)))
    step_raw = centred(splits[13], (STEPS, REQUESTS, H), 1.0, 4.0, ((1, 32), (2, 16)), jnp.float32)
    state_maps = centred(splits[14], (STEPS, REQUESTS, 2, G * N), 0.3, 4.0, ((1, 32),))
    queries = draw_queries(jax.random.fold_in(splits[17], 71), 0)
    new_entries = draw_new_entries(jax.random.fold_in(splits[17], 71), 0)
    return {"scan_state": scan_state, "decay_rate": decay_rate, "step_bias": step_bias, "skip_gain": skip_gain, "norm_gain": norm_gain, "page_pool": page_pool, "old_table": old_table, "new_table": new_table, "request_source": request_source, "head_source": head_source, "context_lengths": context_lengths, "mixer_input": mixer_input, "mixer_gate": mixer_gate, "step_raw": step_raw, "state_maps": state_maps, "queries": queries, "new_entries": new_entries}


EPSILON = 1e-05
HIGH = lax.Precision.HIGHEST

def mixer_request(state_now, inputs_now, gates_now, raw_steps, maps_now, head_bias, head_rate, head_skip, head_gain, member):
    step_size = jax.nn.softplus(raw_steps + head_bias)
    decay = jnp.exp(-head_rate * step_size)
    head_maps = jnp.einsum('hg,sgn->shn', member, maps_now, precision=HIGH)
    state_now = decay[:, None, None] * state_now + (step_size[:, None] * inputs_now)[:, :, None] * head_maps[0][:, None, :]
    mixed = jnp.einsum('hpn,hn->hp', state_now, head_maps[1], precision=HIGH) + head_skip[:, None] * inputs_now
    gated = mixed * jax.nn.silu(gates_now)
    squares = jnp.dot(lax.optimization_barrier(jnp.sum(gated * gated, axis=1)), member, precision=HIGH)
    scale = lax.rsqrt(jnp.dot(member, squares / (H // G * P_SIZE), precision=HIGH) + EPSILON)
    return (state_now, (gated * scale[:, None] * head_gain).astype(jnp.bfloat16))

def attend_request(arguments):
    page_set, query_row, position = arguments
    entries = page_set.reshape(CONTEXT, 2, KVH, HD).astype(jnp.float32)
    query_heads = query_row.reshape(KVH, QH // KVH, HD).astype(jnp.float32)
    scores = jnp.einsum('gqd,cgd->gqc', query_heads, entries[:, 0], precision=HIGH) * (1.0 / math.sqrt(HD))
    visible = jnp.arange(CONTEXT, dtype=jnp.int32) <= position
    masked = jnp.where(visible[None, None, :], scores, -jnp.inf)
    weights = jnp.exp(masked - lax.optimization_barrier(jnp.max(masked, axis=2, keepdims=True))).astype(jnp.bfloat16)
    totals = lax.optimization_barrier(jnp.sum(weights.astype(jnp.float32), axis=2))
    numerator = jnp.einsum('gqc,cgd->gqd', weights.astype(jnp.float32), entries[:, 1], precision=HIGH)
    return (numerator / totals[:, :, None]).astype(jnp.bfloat16).reshape(QH * HD)

def reference(scan_state, decay_rate, step_bias, skip_gain, norm_gain, page_pool, old_table, new_table, request_source, head_source, context_lengths, mixer_input, mixer_gate, step_raw, state_maps, queries, new_entries):
    group_of = head_source // (H // G)
    member = (group_of[:, None] == jnp.arange(G, dtype=jnp.int32)[None, :]).astype(jnp.float32)
    head_bias = step_bias[head_source]
    head_rate = decay_rate[head_source]
    head_skip = skip_gain[head_source]
    head_gain = norm_gain[head_source]

    def one_request(index):
        state_now = scan_state[request_source[index]][head_source]
        outputs = []
        for decode_step in range(STEPS):
            inputs_now = mixer_input[decode_step, index].astype(jnp.float32).reshape(H, P_SIZE)
            gates_now = mixer_gate[decode_step, index].astype(jnp.float32).reshape(H, P_SIZE)
            maps_now = state_maps[decode_step, index].astype(jnp.float32).reshape(2, G, N)
            state_now, output = mixer_request(state_now, inputs_now, gates_now, step_raw[decode_step, index], maps_now, head_bias, head_rate, head_skip, head_gain, member)
            outputs.append(output.reshape(H * P_SIZE))
        return (state_now, jnp.stack(outputs))
    final_state, mixed = lax.map(one_request, jnp.arange(REQUESTS, dtype=jnp.int32))
    mixer_out = jnp.transpose(mixed, (1, 0, 2))
    tensors = jnp.arange(N_TP, dtype=jnp.int32)
    old_owner = request_source // RQ_DEV
    old_index = (old_owner[:, None, None] * N_TP + tensors[None, None, :]) * PG_DEV + old_table[request_source]
    pages = page_pool[old_index.astype(jnp.int32)]
    new_owner = jnp.arange(REQUESTS, dtype=jnp.int32) // RQ_DEV
    new_index = (new_owner[:, None, None] * N_TP + tensors[None, None, :]) * PG_DEV + new_table
    lengths = context_lengths[request_source]
    rows = jnp.arange(REQUESTS, dtype=jnp.int32)
    outputs = []
    for decode_step in range(STEPS):
        position = lengths + decode_step
        logical = position // PAGE
        pages = pages.at[rows, logical // N_TP, logical % N_TP, position % PAGE].set(new_entries[decode_step])
        outputs.append(lax.map(attend_request, (pages, queries[decode_step], position)))
    attention = jnp.stack(outputs)
    final_pool = jnp.zeros_like(page_pool).at[new_index.reshape(-1).astype(jnp.int32)].set(pages.reshape(-1, PAGE, KVW))
    return (mixer_out, attention, final_state, final_pool)
```

```python
import math

import jax
import jax.numpy as jnp
from jax import lax
from jax.experimental import pallas as pl
from jax.experimental.pallas import tpu as pltpu
from jax.sharding import PartitionSpec as P

MESH = pl.DeviceIdType.MESH
HIGH = lax.Precision.HIGHEST
F32 = jnp.float32
BF16 = jnp.bfloat16
I32 = jnp.int32

P_SIZE = 64
N = 128
G = 8
QH = 64
KVH = 8
HD = 128
PAGE = 16
STEPS = 2
ROWS = 4
PGS = 4
MV = 2
HPD = 8
HMV = 4
HEADS_PER_GROUP = 16
GROUP_CHANNELS = 1024
KVW = 2048
SLOTS = ROWS * PGS
SI = STEPS * ROWS
CH = HPD * P_SIZE
NEG = -1e30
EPSILON = 1e-05

T_AR, T_AL, T_HEAD, T_BR, T_BL, T_ROW = 0, 4, 8, 16, 18, 20
T_OWNPG, T_RECVPG, T_ISOWN, T_INV, T_GROUP, T_LEN, T_PAR = 24, 40, 56, 60, 76, 84, 88


def dot_nt(a, b, precision=None):
    return lax.dot_general(
        a, b, (((1,), (1,)), ((), ())), precision=precision, preferred_element_type=F32
    )


def choose(source, base, count, block, most):
    picks = [jnp.int32(0)] * most
    seen = jnp.int32(0)
    for i in range(count):
        v = source[base + i]
        hit = v // count == block
        for k in range(most):
            picks[k] = jnp.where(hit & (seen == k), v - block * count, picks[k])
        seen = seen + hit.astype(I32)
    return picks


def kernel(ntp, nreq, *refs):
    (
        state_hbm, gain_hbm, pool_hbm, x_hbm, gate_hbm, maps_hbm, q_hbm, entry_hbm,
        raw_hbm, rate_h, bias_h, skip_h, old_h, new_h, rsrc_h, hsrc_h, ctx_h,
        mixer_hbm, attn_hbm, state_out, pool_out,
        own, a_send, a_recv, rowbuf, b_send, b_recv, pool_v, c_send, c_recv, newp, fin_pool, fin_state,
        gain_in, x_in, gate_in, maps_in, q_in, entry_in,
        p_own, p_recv, p_gain, p_scal, slot_scal, dt_v, decay_v, raw_t,
        xf, xpad, x_t, qf, ef, maps_f, maps_g, c_rows, outer, member, skip_row, gain_row, stash, ybuf,
        vis, x_send, x_recv, l_send, l_recv, s_send, s_recv, mixer_v, attn_v, raw_in,
        rate_s, bias_s, skip_s, old_s, new_s, rsrc, hsrc, ctx, tab,
        in_sem, scalar_sem, a_ss, a_rs, p_ss, p_rs, b_ss, b_rs, c_ss, c_rs, x_ss, x_rs, l_ss, l_rs, s_ss, s_rs, out_sem,
    ) = refs
    share = QH // ntp
    xrows = share * SI
    t = lax.axis_index("tp")
    r = lax.axis_index("req")
    t_right, t_left = lax.rem(t + 1, ntp), lax.rem(t + ntp - 1, ntp)
    r_right, r_left = lax.rem(r + 1, nreq), lax.rem(r + nreq - 1, nreq)
    dev = {"tr": (r, t_right), "tl": (r, t_left), "rr": (r_right, t), "rl": (r_left, t)}

    scalars = [
        pltpu.make_async_copy(src, dst, scalar_sem.at[k])
        for k, (src, dst) in enumerate(
            (
                (hsrc_h, hsrc), (rsrc_h, rsrc), (old_h, old_s), (ctx_h, ctx), (new_h, new_s),
                (rate_h, rate_s), (bias_h, bias_s), (skip_h, skip_s),
            )
        )
    ]
    loads = [
        pltpu.make_async_copy(state_hbm, own.at[:, pl.ds(0, HPD)], in_sem.at[0]),
        pltpu.make_async_copy(pool_hbm, pool_v, in_sem.at[1]),
        pltpu.make_async_copy(gain_hbm, gain_in, in_sem.at[2]),
        pltpu.make_async_copy(x_hbm, x_in, in_sem.at[3]),
        pltpu.make_async_copy(gate_hbm, gate_in, in_sem.at[4]),
        pltpu.make_async_copy(maps_hbm, maps_in, in_sem.at[5]),
        pltpu.make_async_copy(q_hbm, q_in, in_sem.at[6]),
        pltpu.make_async_copy(entry_hbm, entry_in, in_sem.at[7]),
        pltpu.make_async_copy(raw_hbm, raw_in, in_sem.at[8]),
    ]
    for c in scalars + loads:
        c.start()

    barrier = pltpu.get_barrier_semaphore()
    for name in ("rr", "rl"):
        pl.semaphore_signal(barrier, inc=1, device_id=dev[name], device_id_type=MESH)

    def greet(k, _):
        pl.semaphore_signal(
            barrier, inc=1, device_id=(r, lax.rem(t + k, ntp)), device_id_type=MESH
        )
        return 0

    lax.fori_loop(1, ntp, greet, 0)

    with jax.named_scope("scalars"):
        for c in scalars:
            c.wait()
    for k, v in enumerate(choose(hsrc, t_right * HPD, HPD, t, HMV)):
        tab[T_AR + k] = v
    for k, v in enumerate(choose(hsrc, t_left * HPD, HPD, t, HMV)):
        tab[T_AL + k] = v
    for k, v in enumerate(choose(rsrc, r_right * ROWS, ROWS, r, MV)):
        tab[T_BR + k] = v
    for k, v in enumerate(choose(rsrc, r_left * ROWS, ROWS, r, MV)):
        tab[T_BL + k] = v
    lefts, rights = jnp.int32(0), jnp.int32(0)
    for j in range(HPD):
        v = hsrc[t * HPD + j]
        far = v // HPD - t
        place = jnp.where(far == 0, v - t * HPD, jnp.where(far < 0, HPD + lefts, HPD + HMV + rights))
        tab[T_HEAD + j] = jnp.clip(place, 0, HPD + 2 * HMV - 1)
        tab[T_PAR + j] = jnp.clip(v - t * HPD + HPD, 0, 3 * HPD - 1)
        tab[T_GROUP + j] = v // HEADS_PER_GROUP
        lefts = lefts + (far < 0).astype(I32)
        rights = rights + (far > 0).astype(I32)
    lefts, rights = jnp.int32(0), jnp.int32(0)
    for i in range(ROWS):
        v = rsrc[r * ROWS + i]
        far = v // ROWS - r
        here = jnp.where(far == 0, v - r * ROWS, 0)
        away = jnp.where(far < 0, lefts, MV + rights)
        away = jnp.clip(jnp.where(far == 0, 0, away), 0, 2 * MV - 1)
        tab[T_ROW + i] = jnp.where(far == 0, here, ROWS + away)
        tab[T_ISOWN + i] = (far == 0).astype(I32)
        tab[T_LEN + i] = ctx[v]
        for g in range(PGS):
            tab[T_OWNPG + i * PGS + g] = old_s[here, 0, g]
            tab[T_RECVPG + i * PGS + g] = away * PGS + g
        lefts = lefts + (far < 0).astype(I32)
        rights = rights + (far > 0).astype(I32)

    loads[0].wait()

    def pack_a(n, _):
        d, k, q = n // (HMV * ROWS), (n // ROWS) % HMV, n % ROWS
        a_send[d, k, q] = own[q, tab[T_AR + d * HMV + k]].astype(BF16)
        return 0

    lax.fori_loop(0, 2 * HMV * ROWS, pack_a, 0)

    loads[2].wait()
    sub = lax.broadcasted_iota(I32, (HPD, N), 0)
    lane = lax.broadcasted_iota(I32, (HPD, N), 1)
    p_own[0:HPD, 0:P_SIZE] = gain_in[...]
    wide = p_own[0:HPD, :]
    p_own[0:HPD, :] = jnp.where(lane < P_SIZE, wide, pltpu.roll(wide, P_SIZE, 1))
    scal = jnp.zeros((HPD, N), F32)
    for h in range(HPD):
        for place, ref in enumerate((bias_s, rate_s, skip_s)):
            scal = jnp.where((sub == h) & (lane == place), ref[h], scal)
    p_own[HPD : 2 * HPD, :] = scal

    with jax.named_scope("entry_barrier"):
        pl.semaphore_wait(barrier, ntp + 1)

    def send(src, dst, ss, rs, to):
        return pltpu.make_async_remote_copy(
            src_ref=src, dst_ref=dst, send_sem=ss, recv_sem=rs, device_id=to, device_id_type=MESH
        )

    a_cp = [
        send(a_send.at[d], a_recv.at[d], a_ss.at[d], a_rs.at[d], dev[("tr", "tl")[d]])
        for d in range(2)
    ]
    p_cp = [
        send(p_own, p_recv.at[d], p_ss.at[d], p_rs.at[d], dev[("tr", "tl")[d]]) for d in range(2)
    ]
    for c in p_cp + a_cp:
        c.start()

    loads[1].wait()

    def pack_c(n, _):
        d, k, g = n // (MV * PGS), (n // PGS) % MV, n % PGS
        c_send[n] = pool_v[old_s[tab[T_BR + d * MV + k], 0, g]]
        return 0

    c_cp = []
    for d in range(2):
        lax.fori_loop(d * MV * PGS, (d + 1) * MV * PGS, pack_c, 0)
        part = pl.ds(d * MV * PGS, MV * PGS)
        c = send(c_send.at[part], c_recv.at[part], c_ss.at[d], c_rs.at[d], dev[("rr", "rl")[d]])
        c.start()
        c_cp.append(c)

    for i in range(SLOTS):
        found = jnp.int32(0)
        for e in range(SLOTS):
            found = jnp.where(new_s[e // PGS, 0, e % PGS] == i, e, found)
        tab[T_INV + i] = found
    for c in loads[3:]:
        c.wait()
    xpad[...] = jnp.zeros_like(xpad)
    for s in range(STEPS):
        part = slice(s * ROWS, (s + 1) * ROWS)
        xf[0, part, :] = x_in[s].astype(F32)
        xf[1, part, :] = gate_in[s].astype(F32)
        qf[part, :] = q_in[s].astype(F32)
        ef[part, :] = entry_in[s].astype(F32)
        for i in range(ROWS):
            row = 2 * (s * ROWS + i)
            maps_f[row : row + 2, :] = maps_in[s, i].astype(F32)
    for g in range(G):
        maps_g[g] = maps_f[:, g * N : (g + 1) * N]
    for s in range(STEPS):
        xpad[s * ROWS : (s + 1) * ROWS, 0:HPD] = raw_in[s]
    raw_t[...] = xpad[:, 0:N].T[0:HPD, :]
    xpad[0:SI, :] = xf[0]
    for m in range(CH // N):
        x_t[m * N : (m + 1) * N, :] = xpad[:, m * N : (m + 1) * N].T

    rowid = lax.broadcasted_iota(I32, (QH, ROWS * PGS * PAGE), 0)
    colid = lax.broadcasted_iota(I32, (QH, ROWS * PGS * PAGE), 1)
    row_i = rowid % ROWS
    limit = (rowid // ROWS) % STEPS
    for i in range(ROWS):
        limit = limit + jnp.where(row_i == i, tab[T_LEN + i], 0)
    place = ((colid // PAGE) % PGS * ntp + t) * PAGE + colid % PAGE
    seen = (row_i == colid // (PGS * PAGE)) & (place <= limit)
    vis[...] = jnp.where(seen, 1.0, 0.0)

    with jax.named_scope("params_arrive"):
        for c in p_cp:
            c.wait_recv()
    for part, buf in enumerate((p_gain, p_scal)):
        rows = slice(part * HPD, (part + 1) * HPD)
        buf[0:HPD, :] = p_recv[0, rows, :]
        buf[HPD : 2 * HPD, :] = p_own[rows, :]
        buf[2 * HPD : 3 * HPD, :] = p_recv[1, rows, :]
    for j in range(HPD):
        slot_scal[j : j + 1, :] = p_scal[pl.ds(tab[T_PAR + j], 1), :]
    bias, rate, skip = (slot_scal[:, k : k + 1] for k in range(3))
    v = raw_t[...] + bias
    dt = jnp.maximum(v, 0.0) + jnp.log1p(jnp.exp(-jnp.abs(v)))
    dt_v[...] = dt
    decay_v[...] = jnp.exp(-rate * dt)
    lane1 = lax.broadcasted_iota(I32, (1, N), 1)
    for m in range(CH // N):
        lanes = slice(m * N, (m + 1) * N)
        first = p_gain[pl.ds(tab[T_PAR + 2 * m], 1), :]
        second = p_gain[pl.ds(tab[T_PAR + 2 * m + 1], 1), :]
        gain_row[:, lanes] = jnp.where(lane1 < P_SIZE, first, second)
        skip_row[:, lanes] = jnp.where(
            lane1 < P_SIZE,
            jnp.broadcast_to(skip[2 * m : 2 * m + 1], (1, N)),
            jnp.broadcast_to(skip[2 * m + 1 : 2 * m + 2], (1, N)),
        )
    lane64 = lax.broadcasted_iota(I32, (P_SIZE, N), 1)

    def prepare(j, _):
        group = tab[T_GROUP + j]
        member[pl.ds(pl.multiple_of(j * P_SIZE, P_SIZE), P_SIZE), :] = jnp.where(
            lane64 == group, 1.0, 0.0
        )
        both = maps_g[group]
        dts = dt_v[pl.ds(j, 1), :]
        cols = x_t[pl.ds(pl.multiple_of(j * P_SIZE, P_SIZE), P_SIZE), :]
        for k in range(SI):
            outer[k, j] = cols[:, k : k + 1] * (dts[:, k : k + 1] * both[2 * k : 2 * k + 1, :])
            c_rows[k, pl.ds(j, 1), :] = both[2 * k + 1 : 2 * k + 2, :]
        return 0

    lax.fori_loop(0, HPD, prepare, 0)

    with jax.named_scope("heads_arrive"):
        for c in a_cp:
            c.wait_recv()

    def take_a(n, _):
        k, q = n // ROWS, n % ROWS
        own[q, HPD + k] = a_recv[k // HMV, k % HMV, q].astype(F32)
        return 0

    lax.fori_loop(0, 2 * HMV * ROWS, take_a, 0)

    def take_own(n, _):
        q, j = n // HPD, n % HPD
        rowbuf[q, j] = own[q, tab[T_HEAD + j]]
        return 0

    lax.fori_loop(0, ROWS * HPD, take_own, 0)

    def pack_b(n, _):
        d, k, j = n // (MV * HPD), (n // HPD) % MV, n % HPD
        b_send[d, k, j] = rowbuf[tab[T_BR + d * MV + k], j].astype(BF16)
        return 0

    lax.fori_loop(0, 2 * MV * HPD, pack_b, 0)
    b_cp = [
        send(b_send.at[d], b_recv.at[d], b_ss.at[d], b_rs.at[d], dev[("rr", "rl")[d]])
        for d in range(2)
    ]

    with jax.named_scope("pages_arrive"):
        for c in c_cp:
            c.wait_recv()
    for c in b_cp:
        c.start()
    offset = lax.broadcasted_iota(I32, (PAGE, KVW), 0)

    def take_page(n, _):
        i, g = n // PGS, n % PGS
        mine = pool_v[tab[T_OWNPG + n]].astype(F32)
        came = c_recv[tab[T_RECVPG + n]].astype(F32)
        page = jnp.where(tab[T_ISOWN + i] == 1, mine, came)
        for s in range(STEPS):
            position = tab[T_LEN + i] + s
            logical = position // PAGE
            hit = (logical % ntp == t) & (logical // ntp == g)
            at = jnp.where(hit, position % PAGE, -1)
            page = jnp.where(offset == at, ef[pl.ds(s * ROWS + i, 1), :], page)
        newp[n] = page.astype(BF16)
        return 0

    lax.fori_loop(0, SLOTS, take_page, 0)

    eye = lax.broadcasted_iota(I32, (xrows, N), 0) == lax.broadcasted_iota(I32, (xrows, N), 1)
    shown = vis[...] > 0.5
    per = QH // KVH
    for g in range(KVH):
        q = jnp.concatenate(
            [qf[:, (g * per + h) * HD : (g * per + h + 1) * HD] for h in range(per)], axis=0
        ).astype(BF16)
        keys = newp[:, :, g * HD : (g + 1) * HD].reshape(SLOTS * PAGE, HD)
        values = newp[:, :, (KVH + g) * HD : (KVH + g + 1) * HD].reshape(SLOTS * PAGE, HD)
        scores = jnp.where(shown, dot_nt(q, keys) * (1.0 / math.sqrt(HD)), NEG)
        peak = jnp.max(scores, axis=1, keepdims=True)
        weights = jnp.where(shown, jnp.exp(scores - peak), 0.0).astype(BF16)
        total = jnp.sum(weights.astype(F32), axis=1, keepdims=True)
        part = jnp.dot(weights, values, preferred_element_type=F32)
        safe = jnp.maximum(total, 1e-30)
        part = (part / safe).astype(BF16)
        lse = jnp.where(total > 0.0, peak + jnp.log(safe), NEG)
        for e in range(per // share):
            rows = slice(e * xrows, (e + 1) * xrows)
            x_send[g * (per // share) + e] = part[rows]
            l_send[g * (per // share) + e] = jnp.sum(
                jnp.where(eye, lse[rows], 0.0), axis=0, keepdims=True
            )

    def x_copy(k):
        to = lax.rem(t + k, ntp)
        return (
            send(x_send.at[to], x_recv.at[k], x_ss.at[k], x_rs.at[k], (r, to)),
            send(l_send.at[to], l_recv.at[k], l_ss.at[k], l_rs.at[k], (r, to)),
        )

    def x_start(k, _):
        for c in x_copy(k):
            c.start()
        return 0

    lax.fori_loop(1, ntp, x_start, 0)
    x_recv[0] = x_send[t]
    l_recv[0] = l_send[t]

    def place_page(n, _):
        fin_pool[n] = newp[tab[T_INV + n]]
        return 0

    lax.fori_loop(0, SLOTS, place_page, 0)
    outs = [pltpu.make_async_copy(fin_pool, pool_out, out_sem.at[0])]
    outs[0].start()

    def x_wait(k, _):
        for c in x_copy(k):
            c.wait_recv()
        return 0

    with jax.named_scope("partials_arrive"):
        lax.fori_loop(1, ntp, x_wait, 0)
    lses = l_recv[...].reshape(ntp, N)
    w = jnp.exp(lses - jnp.max(lses, axis=0, keepdims=True))
    w = w / jnp.sum(w, axis=0, keepdims=True)
    total = jnp.zeros((xrows, HD), F32)
    for k in range(ntp):
        col = jnp.sum(jnp.where(eye, w[k : k + 1, :], 0.0), axis=1, keepdims=True)
        total = total + col * x_recv[k].astype(F32)
    for s in range(STEPS):
        for h in range(share):
            attn_v[s, :, h * HD : (h + 1) * HD] = total[
                h * SI + s * ROWS : h * SI + (s + 1) * ROWS
            ].astype(BF16)
    outs.append(pltpu.make_async_copy(attn_v, attn_hbm, out_sem.at[1]))
    outs[1].start()

    with jax.named_scope("rows_arrive"):
        for c in b_cp:
            c.wait_recv()

    def take_b(n, _):
        k, j = n // HPD, n % HPD
        rowbuf[ROWS + k, j] = b_recv[k // MV, k % MV, j].astype(F32)
        return 0

    lax.fori_loop(0, 2 * MV * HPD, take_b, 0)
    diagonal = lax.broadcasted_iota(I32, (HPD, CH), 0) == (
        lax.broadcasted_iota(I32, (HPD, CH), 1) // P_SIZE
    )
    for i in range(ROWS):

        def step(j, _):
            now = rowbuf[tab[T_ROW + i], j]
            fade = decay_v[pl.ds(j, 1), :]
            for s in range(STEPS):
                k = s * ROWS + i
                now = fade[:, k : k + 1] * now + outer[k, j]
                stash[s, pl.ds(pl.multiple_of(j * P_SIZE, P_SIZE), P_SIZE), :] = now
            fin_state[i, j] = now
            return 0

        lax.fori_loop(0, HPD, step, 0)
        for s in range(STEPS):
            k = s * ROWS + i
            now = stash[s]
            top = now.astype(BF16)
            low = (now - top.astype(F32)).astype(BF16)
            c8 = c_rows[k].astype(BF16)
            y = dot_nt(c8, top) + dot_nt(c8, low)
            ybuf[k : k + 1, :] = jnp.sum(jnp.where(diagonal, y, 0.0), axis=0, keepdims=True)
    outs.append(pltpu.make_async_copy(fin_state, state_out, out_sem.at[2]))
    outs[2].start()

    gate = xf[1]
    gated = (ybuf[...] + skip_row[...] * xf[0]) * (gate / (1.0 + jnp.exp(-gate)))
    s_send[...] = jnp.dot(gated * gated, member[...], precision=HIGH, preferred_element_type=F32)

    def s_copy(k):
        to = lax.rem(t + k, ntp)
        return send(s_send, s_recv.at[k], s_ss.at[k], s_rs.at[k], (r, to))

    def s_start(k, _):
        s_copy(k).start()
        return 0

    lax.fori_loop(1, ntp, s_start, 0)
    s_recv[0] = s_send[...]

    def s_wait(k, _):
        s_copy(k).wait_recv()
        return 0

    with jax.named_scope("squares_arrive"):
        lax.fori_loop(1, ntp, s_wait, 0)
    squares = jnp.sum(s_recv[...], axis=0)
    scale = lax.rsqrt(squares * (1.0 / GROUP_CHANNELS) + EPSILON)
    mixed = gated * dot_nt(scale, member[...], HIGH) * gain_row[...]
    for s in range(STEPS):
        mixer_v[s] = mixed[s * ROWS : (s + 1) * ROWS].astype(BF16)
    outs.append(pltpu.make_async_copy(mixer_v, mixer_hbm, out_sem.at[3]))
    outs[3].start()

    def last(k, _):
        for c in x_copy(k) + (s_copy(k),):
            c.wait_send()
        return 0

    with jax.named_scope("all_sent"):
        for c in a_cp + p_cp + c_cp + b_cp:
            c.wait_send()
        lax.fori_loop(1, ntp, last, 0)
        for c in outs:
            c.wait()


def per_device(ntp, nreq, *arguments):
    (
        scan_state, decay_rate, step_bias, skip_gain, norm_gain, page_pool, old_table, new_table,
        request_source, head_source, context_lengths, mixer_input, mixer_gate, step_raw, state_maps,
        queries, new_entries,
    ) = arguments
    xrows = QH // ntp * SI
    anywhere = pl.BlockSpec(memory_space=pl.ANY)
    dma = pltpu.SemaphoreType.DMA
    scratch = [
        ((ROWS, HPD + 2 * HMV, P_SIZE, N), F32),
        ((2, HMV, ROWS, P_SIZE, N), BF16),
        ((2, HMV, ROWS, P_SIZE, N), BF16),
        ((ROWS + 2 * MV, HPD, P_SIZE, N), F32),
        ((2, MV, HPD, P_SIZE, N), BF16),
        ((2, MV, HPD, P_SIZE, N), BF16),
        ((SLOTS, PAGE, KVW), BF16),
        ((2 * MV * PGS, PAGE, KVW), BF16),
        ((2 * MV * PGS, PAGE, KVW), BF16),
        ((SLOTS, PAGE, KVW), BF16),
        ((SLOTS, PAGE, KVW), BF16),
        ((ROWS, HPD, P_SIZE, N), F32),
        (norm_gain.shape, F32),
        (mixer_input.shape, BF16),
        (mixer_gate.shape, BF16),
        (state_maps.shape, BF16),
        (queries.shape, BF16),
        (new_entries.shape, BF16),
        ((2 * HPD, N), F32),
        ((2, 2 * HPD, N), F32),
        ((3 * HPD, N), F32),
        ((3 * HPD, N), F32),
        ((HPD, N), F32),
        ((HPD, N), F32),
        ((HPD, N), F32),
        ((HPD, N), F32),
        ((2, SI, CH), F32),
        ((N, CH), F32),
        ((CH, N), F32),
        ((SI, QH * HD), F32),
        ((SI, KVW), F32),
        ((2 * SI, G * N), F32),
        ((G, 2 * SI, N), F32),
        ((SI, HPD, N), F32),
        ((SI, HPD, P_SIZE, N), F32),
        ((CH, N), F32),
        ((1, CH), F32),
        ((1, CH), F32),
        ((STEPS, CH, N), F32),
        ((SI, CH), F32),
        ((QH, SLOTS * PAGE), F32),
        ((ntp, xrows, HD), BF16),
        ((ntp, xrows, HD), BF16),
        ((ntp, 1, N), F32),
        ((ntp, 1, N), F32),
        ((SI, N), F32),
        ((ntp, SI, N), F32),
        ((STEPS, ROWS, CH), BF16),
        ((STEPS, ROWS, CH), BF16),
        (step_raw.shape, F32),
    ]
    return pl.pallas_call(
        lambda *refs: kernel(ntp, nreq, *refs),
        out_shape=(
            jax.ShapeDtypeStruct((STEPS, ROWS, CH), BF16),
            jax.ShapeDtypeStruct((STEPS, ROWS, CH), BF16),
            jax.ShapeDtypeStruct(scan_state.shape, F32),
            jax.ShapeDtypeStruct(page_pool.shape, BF16),
        ),
        in_specs=[pl.BlockSpec(memory_space=pltpu.HBM)] * 17,
        out_specs=(anywhere,) * 4,
        scratch_shapes=[pltpu.VMEM(shape, dtype) for shape, dtype in scratch]
        + [
            *[pltpu.SMEM((HPD,), F32) for _ in range(3)],
            *[pltpu.SMEM((ROWS, 1, PGS), I32) for _ in range(2)],
            *[pltpu.SMEM(ints.shape, I32) for ints in (request_source, head_source, context_lengths)],
            pltpu.SMEM((128,), I32),
            dma((9,)),
            dma((8,)),
            *[dma((2,)) for _ in range(8)],
            *[dma((ntp,)) for _ in range(6)],
            dma((4,)),
        ],
        compiler_params=pltpu.CompilerParams(
            collective_id=0, has_side_effects=True, vmem_limit_bytes=63 * 2**20
        ),
        name="decode",
    )(
        scan_state, norm_gain, page_pool, mixer_input, mixer_gate, state_maps, queries, new_entries,
        step_raw, decay_rate, step_bias, skip_gain, old_table.transpose(0, 2, 1), new_table.transpose(0, 2, 1),
        request_source, head_source, context_lengths,
    )


def solution(mesh):
    ntp, nreq = mesh.shape["tp"], mesh.shape["req"]
    return jax.shard_map(
        lambda *arguments: per_device(ntp, nreq, *arguments),
        mesh=mesh,
        in_specs=(
            P("req", "tp", None, None),
            P("tp"),
            P("tp"),
            P("tp"),
            P("tp", None),
            P(("req", "tp"), None, None),
            P("req", None, "tp"),
            P("req", None, "tp"),
            P(),
            P(),
            P(),
            P(None, "req", "tp"),
            P(None, "req", "tp"),
            P(None, "req", "tp"),
            P(None, "req", None, None),
            P(None, "req", None),
            P(None, "req", None),
        ),
        out_specs=(
            P(None, "req", "tp"),
            P(None, "req", "tp"),
            P("req", "tp", None, None),
            P(("req", "tp"), None, None),
        ),
        check_vma=False,
    )
```

```python
import math

import jax
import jax.numpy as jnp
from jax import lax
from jax.experimental import pallas as pl
from jax.experimental.pallas import tpu as pltpu
from jax.sharding import PartitionSpec as P

MESH = pl.DeviceIdType.MESH
HIGH = lax.Precision.HIGHEST
F32 = jnp.float32
BF16 = jnp.bfloat16
I32 = jnp.int32

P_SIZE = 64
N = 128
G = 8
QH = 64
KVH = 8
HD = 128
PAGE = 16
STEPS = 2
ROWS = 4
PGS = 4
MV = 2
HPD = 8
HMV = 4
HEADS_PER_GROUP = 16
GROUP_CHANNELS = 1024
KVW = 2048
SLOTS = ROWS * PGS
SI = STEPS * ROWS
CH = HPD * P_SIZE
NEG = -1e30
EPSILON = 1e-05

T_AR, T_AL, T_HEAD, T_BR, T_BL, T_ROW = 0, 4, 8, 16, 18, 20
T_OWNPG, T_RECVPG, T_ISOWN, T_INV, T_GROUP, T_LEN, T_PAR = 24, 40, 56, 60, 76, 84, 88
T_RR, T_RL, T_REC = 96, 98, 100
PIECES = 4
REC, REC_X, REC_GATE, REC_MAPS, REC_RAW = 16, 0, 2, 4, 12


def dot_nt(a, b, precision=None):
    return lax.dot_general(
        a, b, (((1,), (1,)), ((), ())), precision=precision, preferred_element_type=F32
    )


def choose(source, base, count, block, most):
    picks = [jnp.int32(0)] * most
    seen = jnp.int32(0)
    for i in range(count):
        v = source[base + i]
        hit = v // count == block
        for k in range(most):
            picks[k] = jnp.where(hit & (seen == k), v - block * count, picks[k])
        seen = seen + hit.astype(I32)
    return picks


def choose_slots(source, base, count, block, most):
    picks = [jnp.int32(0)] * most
    seen = jnp.int32(0)
    for i in range(count):
        hit = source[base + i] // count == block
        for k in range(most):
            picks[k] = jnp.where(hit & (seen == k), i, picks[k])
        seen = seen + hit.astype(I32)
    return picks


def kernel(ntp, nreq, *refs):
    (
        state_hbm, gain_hbm, pool_hbm, x_hbm, gate_hbm, maps_hbm, q_hbm, entry_hbm,
        raw_hbm, rate_h, bias_h, skip_h, old_h, new_h, rsrc_h, hsrc_h, ctx_h,
        mixer_hbm, attn_hbm, state_out, pool_out,
        own, a_send, a_recv, rowbuf, b_send, b_recv, pool_v, c_send, c_recv, newp, fin_pool, fin_state,
        gain_in, x_in, gate_in, maps_in, q_in, entry_in,
        p_own, p_recv, p_gain, p_scal, slot_scal, dt_v, decay_v, raw_t,
        xf, rec, r_send, r_recv, recf, xpad, x_t, qf, ef, maps_g, c_rows, outer, member, skip_row, gain_row,
        stash, ybuf, vis, x_send, l_send, x_pair, l_pair, xc_send, xc_recv, lc_send, lc_recv, lses_v, s_send, s_recv, m_send, m_recv, m_all,
        mixer_v, attn_v, raw_in,
        rate_s, bias_s, skip_s, old_s, new_s, rsrc, hsrc, ctx, tab,
        in_sem, scalar_sem, r_ss, r_rs, m_ss, m_rs, a_ss, a_rs, p_ss, p_rs, b_ss, b_rs, c_ss, c_rs, pair_ss, pair_rs, x_ss, x_rs, l_ss, l_rs, s_ss, s_rs, out_sem,
    ) = refs
    share = QH // ntp
    xrows = share * SI
    t = lax.axis_index("tp")
    r = lax.axis_index("req")
    t_right, t_left = lax.rem(t + 1, ntp), lax.rem(t + ntp - 1, ntp)
    r_right, r_left = lax.rem(r + 1, nreq), lax.rem(r + nreq - 1, nreq)
    dev = {"tr": (r, t_right), "tl": (r, t_left), "rr": (r_right, t), "rl": (r_left, t)}

    barrier = pltpu.get_barrier_semaphore()
    for name in ("rr", "rl"):
        pl.semaphore_signal(barrier, inc=1, device_id=dev[name], device_id_type=MESH)

    def peer(k):
        core, y_hi = (t + k) % 2, (t // 2 + k // 2) % 2
        return (t // 4 + k // 4) % (ntp // 4) * 4 + y_hi * 2 + core

    def each_peer(act):
        def far(n, _):
            act(n // 2 * 4 + 2 + n % 2)
            return 0

        def near(n, _):
            act(n // 2 * 4 + n % 2)
            return 0

        lax.fori_loop(0, ntp // 2, far, 0)
        lax.fori_loop(1, ntp // 2, near, 0)

    def greet(k):
        pl.semaphore_signal(barrier, inc=1, device_id=(r, peer(k)), device_id_type=MESH)

    each_peer(greet)

    scalars = [
        pltpu.make_async_copy(src, dst, scalar_sem.at[k])
        for k, (src, dst) in enumerate(
            (
                (hsrc_h, hsrc), (rsrc_h, rsrc), (old_h, old_s), (ctx_h, ctx), (new_h, new_s),
                (rate_h, rate_s), (bias_h, bias_s), (skip_h, skip_s),
            )
        )
    ]
    loads = [
        pltpu.make_async_copy(state_hbm, own.at[:, pl.ds(0, HPD)], in_sem.at[0]),
        pltpu.make_async_copy(pool_hbm, pool_v, in_sem.at[1]),
        pltpu.make_async_copy(gain_hbm, gain_in, in_sem.at[2]),
        pltpu.make_async_copy(x_hbm, x_in, in_sem.at[3]),
        pltpu.make_async_copy(gate_hbm, gate_in, in_sem.at[4]),
        pltpu.make_async_copy(maps_hbm, maps_in, in_sem.at[5]),
        pltpu.make_async_copy(q_hbm, q_in, in_sem.at[6]),
        pltpu.make_async_copy(entry_hbm, entry_in, in_sem.at[7]),
        pltpu.make_async_copy(raw_hbm, raw_in, in_sem.at[8]),
    ]
    for c in scalars + loads:
        c.start()

    with jax.named_scope("scalars"):
        for c in scalars:
            c.wait()
    for k, v in enumerate(choose(hsrc, t_right * HPD, HPD, t, HMV)):
        tab[T_AR + k] = v
    for k, v in enumerate(choose(hsrc, t_left * HPD, HPD, t, HMV)):
        tab[T_AL + k] = v

    loads[0].wait()

    def pack_a(n, _):
        d, k, q = n // (HMV * ROWS), (n // ROWS) % HMV, n % ROWS
        a_send[d, k, q] = own[q, tab[T_AR + d * HMV + k]].astype(BF16)
        return 0

    lax.fori_loop(0, 2 * HMV * ROWS, pack_a, 0)

    loads[2].wait()
    sub = lax.broadcasted_iota(I32, (HPD, N), 0)
    lane = lax.broadcasted_iota(I32, (HPD, N), 1)
    p_own[0:HPD, 0:P_SIZE] = gain_in[...]
    wide = p_own[0:HPD, :]
    p_own[0:HPD, :] = jnp.where(lane < P_SIZE, wide, pltpu.roll(wide, P_SIZE, 1))
    scal = jnp.zeros((HPD, N), F32)
    for h in range(HPD):
        for place, ref in enumerate((bias_s, rate_s, skip_s)):
            scal = jnp.where((sub == h) & (lane == place), ref[h], scal)
    p_own[HPD : 2 * HPD, :] = scal

    with jax.named_scope("entry_barrier"):
        pl.semaphore_wait(barrier, ntp + 1)

    def send(src, dst, ss, rs, to):
        return pltpu.make_async_remote_copy(
            src_ref=src, dst_ref=dst, send_sem=ss, recv_sem=rs, device_id=to, device_id_type=MESH
        )

    a_cp = [
        send(a_send.at[d], a_recv.at[d], a_ss.at[d], a_rs.at[d], dev[("tr", "tl")[d]])
        for d in range(2)
    ]
    p_cp = [
        send(p_own, p_recv.at[d], p_ss.at[d], p_rs.at[d], dev[("tr", "tl")[d]]) for d in range(2)
    ]
    for c in p_cp + a_cp:
        c.start()

    for k, v in enumerate(choose(rsrc, r_right * ROWS, ROWS, r, MV)):
        tab[T_BR + k] = v
    for k, v in enumerate(choose(rsrc, r_left * ROWS, ROWS, r, MV)):
        tab[T_BL + k] = v
    for k, v in enumerate(choose_slots(rsrc, r * ROWS, ROWS, r_right, MV)):
        tab[T_RR + k] = v
    for k, v in enumerate(choose_slots(rsrc, r * ROWS, ROWS, r_left, MV)):
        tab[T_RL + k] = v
    records = [jnp.int32(0)] * ROWS
    for block, base in ((r_left, ROWS), (r, 0), (r_right, ROWS + MV)):
        rank = jnp.int32(0)
        for i in range(ROWS):
            v = rsrc[block * ROWS + i]
            hit = v // ROWS == r
            where = jnp.clip(rank, 0, MV - 1) + base if base else i
            for q in range(ROWS):
                records[q] = jnp.where(hit & (v - r * ROWS == q), where, records[q])
            rank = rank + hit.astype(I32)
    for q in range(ROWS):
        tab[T_REC + q] = records[q]
    lefts, rights = jnp.int32(0), jnp.int32(0)
    for j in range(HPD):
        v = hsrc[t * HPD + j]
        far = v // HPD - t
        place = jnp.where(far == 0, v - t * HPD, jnp.where(far < 0, HPD + lefts, HPD + HMV + rights))
        tab[T_HEAD + j] = jnp.clip(place, 0, HPD + 2 * HMV - 1)
        tab[T_PAR + j] = jnp.clip(v - t * HPD + HPD, 0, 3 * HPD - 1)
        tab[T_GROUP + j] = v // HEADS_PER_GROUP
        lefts = lefts + (far < 0).astype(I32)
        rights = rights + (far > 0).astype(I32)
    lefts, rights = jnp.int32(0), jnp.int32(0)
    for i in range(ROWS):
        v = rsrc[r * ROWS + i]
        far = v // ROWS - r
        here = jnp.where(far == 0, v - r * ROWS, 0)
        away = jnp.where(far < 0, lefts, MV + rights)
        away = jnp.clip(jnp.where(far == 0, 0, away), 0, 2 * MV - 1)
        tab[T_ROW + i] = jnp.where(far == 0, here, ROWS + away)
        tab[T_ISOWN + i] = (far == 0).astype(I32)
        tab[T_LEN + i] = ctx[v]
        for g in range(PGS):
            tab[T_OWNPG + i * PGS + g] = old_s[here, 0, g]
            tab[T_RECVPG + i * PGS + g] = away * PGS + g
        lefts = lefts + (far < 0).astype(I32)
        rights = rights + (far > 0).astype(I32)

    for c in loads[3:6] + loads[8:9]:
        c.wait()
    xpad[...] = jnp.zeros_like(xpad)
    rec[...] = jnp.zeros_like(rec)
    for s in range(STEPS):
        xpad[s * ROWS : (s + 1) * ROWS, 0:HPD] = raw_in[s]
        xf[0, s * ROWS : (s + 1) * ROWS, :] = x_in[s].astype(F32)
        xf[1, s * ROWS : (s + 1) * ROWS, :] = gate_in[s].astype(F32)
    for i in range(ROWS):
        parts = [xf[0, k : k + 1, :] for k in (i, ROWS + i)]
        parts += [xf[1, k : k + 1, :] for k in (i, ROWS + i)]
        for s in range(STEPS):
            maps = maps_in[s, i].astype(F32)
            for bc in range(2):
                parts += [maps[bc : bc + 1, h * CH : (h + 1) * CH] for h in range(2)]
        raws = jnp.concatenate([xpad[i : i + 1, 0:N], xpad[ROWS + i : ROWS + i + 1, 0:N]], axis=1)
        rest = jnp.concatenate([raws, jnp.zeros((1, CH - 2 * N), F32)], axis=1)
        for _ in range(3):
            top = rest.astype(BF16).astype(F32)
            parts.append(top)
            rest = rest - top
        parts.append(rest)
        rec[i] = jnp.concatenate(parts, axis=0).astype(BF16)
    for d in range(2):
        for k in range(MV):
            r_send[d, k] = rec[tab[T_RR + d * MV + k]]

    r_cp = [
        send(r_send.at[d], r_recv.at[d], r_ss.at[d], r_rs.at[d], dev[("rr", "rl")[d]])
        for d in range(2)
    ]
    for c in r_cp:
        c.start()

    loads[1].wait()

    def pack_c(n, _):
        d, k, g = n // (MV * PGS), (n // PGS) % MV, n % PGS
        c_send[n] = pool_v[old_s[tab[T_BR + d * MV + k], 0, g]]
        return 0

    lax.fori_loop(0, 2 * MV * PGS, pack_c, 0)

    c_cp = []
    for d in range(2):
        part = pl.ds(d * MV * PGS, MV * PGS)
        c_cp.append(
            send(c_send.at[part], c_recv.at[part], c_ss.at[d], c_rs.at[d], dev[("rr", "rl")[d]])
        )
    for c in c_cp:
        c.start()

    for i in range(SLOTS):
        found = jnp.int32(0)
        for e in range(SLOTS):
            found = jnp.where(new_s[e // PGS, 0, e % PGS] == i, e, found)
        tab[T_INV + i] = found
    for c in loads[6:8]:
        c.wait()
    for s in range(STEPS):
        part = slice(s * ROWS, (s + 1) * ROWS)
        qf[part, :] = q_in[s].astype(F32)
        ef[part, :] = entry_in[s].astype(F32)

    rowid = lax.broadcasted_iota(I32, (QH, ROWS * PGS * PAGE), 0)
    colid = lax.broadcasted_iota(I32, (QH, ROWS * PGS * PAGE), 1)
    row_i = rowid % ROWS
    limit = (rowid // ROWS) % STEPS
    for i in range(ROWS):
        limit = limit + jnp.where(row_i == i, tab[T_LEN + i], 0)
    place = ((colid // PAGE) % PGS * ntp + t) * PAGE + colid % PAGE
    seen = (row_i == colid // (PGS * PAGE)) & (place <= limit)
    vis[...] = jnp.where(seen, 1.0, 0.0)

    with jax.named_scope("params_arrive"):
        for c in p_cp + r_cp:
            c.wait_recv()
    for part, buf in enumerate((p_gain, p_scal)):
        rows = slice(part * HPD, (part + 1) * HPD)
        buf[0:HPD, :] = p_recv[0, rows, :]
        buf[HPD : 2 * HPD, :] = p_own[rows, :]
        buf[2 * HPD : 3 * HPD, :] = p_recv[1, rows, :]
    for j in range(HPD):
        slot_scal[j : j + 1, :] = p_scal[pl.ds(tab[T_PAR + j], 1), :]
    bias, rate, skip = (slot_scal[:, k : k + 1] for k in range(3))
    for q in range(ROWS):
        at = tab[T_REC + q]
        mine = rec[jnp.minimum(at, ROWS - 1)].astype(F32)
        away = jnp.maximum(at - ROWS, 0)
        came = r_recv[away // MV, away % MV].astype(F32)
        recf[q] = jnp.where(at < ROWS, mine, came)
    for q in range(ROWS):
        raws = recf[q, REC_RAW : REC_RAW + 1, :]
        for k in range(1, 3):
            raws = raws + recf[q, REC_RAW + k : REC_RAW + k + 1, :]
        for s in range(STEPS):
            k = s * ROWS + q
            xf[0, k : k + 1, :] = recf[q, REC_X + s : REC_X + s + 1, :]
            xf[1, k : k + 1, :] = recf[q, REC_GATE + s : REC_GATE + s + 1, :]
            xpad[k : k + 1, 0:N] = raws[:, s * N : (s + 1) * N]
            for bc in range(2):
                for g in range(G):
                    row = REC_MAPS + (s * 2 + bc) * 2 + g // (G // 2)
                    lanes = slice(g % (G // 2) * N, (g % (G // 2) + 1) * N)
                    maps_g[g, 2 * k + bc : 2 * k + bc + 1, :] = recf[q, row : row + 1, lanes]
    raw_t[...] = xpad[:, 0:N].T[0:HPD, :]
    xpad[0:SI, :] = xf[0]
    for m in range(CH // N):
        x_t[m * N : (m + 1) * N, :] = xpad[:, m * N : (m + 1) * N].T
    v = raw_t[...] + bias
    dt = jnp.maximum(v, 0.0) + jnp.log1p(jnp.exp(-jnp.abs(v)))
    dt_v[...] = dt
    decay_v[...] = jnp.exp(-rate * dt)
    lane1 = lax.broadcasted_iota(I32, (1, N), 1)
    for m in range(CH // N):
        lanes = slice(m * N, (m + 1) * N)
        first = p_gain[pl.ds(tab[T_PAR + 2 * m], 1), :]
        second = p_gain[pl.ds(tab[T_PAR + 2 * m + 1], 1), :]
        gain_row[:, lanes] = jnp.where(lane1 < P_SIZE, first, second)
        skip_row[:, lanes] = jnp.where(
            lane1 < P_SIZE,
            jnp.broadcast_to(skip[2 * m : 2 * m + 1], (1, N)),
            jnp.broadcast_to(skip[2 * m + 1 : 2 * m + 2], (1, N)),
        )
    lane64 = lax.broadcasted_iota(I32, (P_SIZE, N), 1)

    def prepare(j, _):
        group = tab[T_GROUP + j]
        member[pl.ds(pl.multiple_of(j * P_SIZE, P_SIZE), P_SIZE), :] = jnp.where(
            lane64 % G == group, 1.0, 0.0
        )
        both = maps_g[group]
        dts = dt_v[pl.ds(j, 1), :]
        cols = x_t[pl.ds(pl.multiple_of(j * P_SIZE, P_SIZE), P_SIZE), :]
        for k in range(SI):
            outer[k, j] = cols[:, k : k + 1] * (dts[:, k : k + 1] * both[2 * k : 2 * k + 1, :])
            c_rows[k, pl.ds(j, 1), :] = both[2 * k + 1 : 2 * k + 2, :]
        return 0

    lax.fori_loop(0, HPD, prepare, 0)

    with jax.named_scope("heads_arrive"):
        for c in a_cp:
            c.wait_recv()

    def take_a(n, _):
        k, q = n // ROWS, n % ROWS
        own[q, HPD + k] = a_recv[k // HMV, k % HMV, q].astype(F32)
        return 0

    lax.fori_loop(0, 2 * HMV * ROWS, take_a, 0)

    diagonal = lax.broadcasted_iota(I32, (HPD, CH), 0) == (
        lax.broadcasted_iota(I32, (HPD, CH), 1) // P_SIZE
    )
    for i in range(ROWS):

        def step(j, _):
            now = own[i, tab[T_HEAD + j]]
            fade = decay_v[pl.ds(j, 1), :]
            for s in range(STEPS):
                k = s * ROWS + i
                now = fade[:, k : k + 1] * now + outer[k, j]
                stash[s, pl.ds(pl.multiple_of(j * P_SIZE, P_SIZE), P_SIZE), :] = now
            rowbuf[i, j] = now
            return 0

        lax.fori_loop(0, HPD, step, 0)
        for s in range(STEPS):
            k = s * ROWS + i
            now = stash[s]
            top = now.astype(BF16)
            low = (now - top.astype(F32)).astype(BF16)
            c8 = c_rows[k].astype(BF16)
            y = dot_nt(c8, top) + dot_nt(c8, low)
            ybuf[k : k + 1, :] = jnp.sum(jnp.where(diagonal, y, 0.0), axis=0, keepdims=True)

    gate = xf[1]
    gated = (ybuf[...] + skip_row[...] * xf[0]) * (gate / (1.0 + jnp.exp(-gate)))
    packed = sub == lane // G
    squares = jnp.dot(gated * gated, member[...], precision=HIGH, preferred_element_type=F32)
    s_send[...] = jnp.sum(jnp.where(packed, squares, 0.0), axis=0, keepdims=True)

    def s_copy(k):
        return send(s_send, s_recv.at[k], s_ss.at[k], s_rs.at[k], (r, peer(k)))

    each_peer(lambda k: s_copy(k).start())
    s_recv[0] = s_send[...]

    def pack_b(n, _):
        d, k, j = n // (MV * HPD), (n // HPD) % MV, n % HPD
        b_send[d, k, j] = rowbuf[tab[T_BR + d * MV + k], j].astype(BF16)
        return 0

    lax.fori_loop(0, 2 * MV * HPD, pack_b, 0)
    b_cp = [
        send(b_send.at[d], b_recv.at[d], b_ss.at[d], b_rs.at[d], dev[("rr", "rl")[d]])
        for d in range(2)
    ]

    for c in b_cp:
        c.start()

    with jax.named_scope("pages_arrive"):
        for c in c_cp:
            c.wait_recv()

    offset = lax.broadcasted_iota(I32, (PAGE, KVW), 0)

    def take_page(n, _):
        i, g = n // PGS, n % PGS
        mine = pool_v[tab[T_OWNPG + n]].astype(F32)
        came = c_recv[tab[T_RECVPG + n]].astype(F32)
        page = jnp.where(tab[T_ISOWN + i] == 1, mine, came)
        for s in range(STEPS):
            position = tab[T_LEN + i] + s
            logical = position // PAGE
            hit = (logical % ntp == t) & (logical // ntp == g)
            at = jnp.where(hit, position % PAGE, -1)
            page = jnp.where(offset == at, ef[pl.ds(s * ROWS + i, 1), :], page)
        newp[n] = page.astype(BF16)
        return 0

    lax.fori_loop(0, SLOTS, take_page, 0)

    eye = lax.broadcasted_iota(I32, (xrows, N), 0) == lax.broadcasted_iota(I32, (xrows, N), 1)
    shown = vis[...] > 0.5
    per = QH // KVH
    for g in range(KVH):
        q = jnp.concatenate(
            [qf[:, (g * per + h) * HD : (g * per + h + 1) * HD] for h in range(per)], axis=0
        ).astype(BF16)
        keys = newp[:, :, g * HD : (g + 1) * HD].reshape(SLOTS * PAGE, HD)
        values = newp[:, :, (KVH + g) * HD : (KVH + g + 1) * HD].reshape(SLOTS * PAGE, HD)
        scores = jnp.where(shown, dot_nt(q, keys) * (1.0 / math.sqrt(HD)), NEG)
        peak = jnp.max(scores, axis=1, keepdims=True)
        weights = jnp.where(shown, jnp.exp(scores - peak), 0.0).astype(BF16)
        total = jnp.sum(weights.astype(F32), axis=1, keepdims=True)
        part = jnp.dot(weights, values, preferred_element_type=F32)
        safe = jnp.maximum(total, 1e-30)
        part = (part / safe).astype(BF16)
        lse = jnp.where(total > 0.0, peak + jnp.log(safe), NEG)
        for e in range(per // share):
            rows = slice(e * xrows, (e + 1) * xrows)
            dest = g * (per // share) + e
            x_send[dest % 2, dest // 2] = part[rows]
            l_send[dest % 2, dest // 2] = jnp.sum(
                jnp.where(eye, lse[rows], 0.0), axis=0, keepdims=True
            )

    side = t % 2
    other = (r, t + 1 - 2 * side)
    pair_cp = [
        send(x_send.at[1 - side], x_pair, pair_ss.at[0], pair_rs.at[0], other),
        send(l_send.at[1 - side], l_pair, pair_ss.at[1], pair_rs.at[1], other),
    ]
    for c in pair_cp:
        c.start()

    with jax.named_scope("squares_arrive"):
        each_peer(lambda k: s_copy(k).wait_recv())
    squares = jnp.sum(s_recv[...], axis=0)
    scale = jnp.where(packed, lax.rsqrt(squares * (1.0 / GROUP_CHANNELS) + EPSILON), 0.0)
    mixed = gated * dot_nt(scale, member[...], HIGH) * gain_row[...]
    for q in range(ROWS):
        for s in range(STEPS):
            for m in range(CH // N):
                k = s * ROWS + q
                m_all[q, s * (CH // N) + m : s * (CH // N) + m + 1, :] = mixed[
                    k : k + 1, m * N : (m + 1) * N
                ]
    for d in range(2):
        for k in range(MV):
            m_send[d, k] = m_all[tab[T_BR + d * MV + k]]
    m_cp = [
        send(m_send.at[d], m_recv.at[d], m_ss.at[d], m_rs.at[d], dev[("rr", "rl")[d]])
        for d in range(2)
    ]
    for c in m_cp:
        c.start()

    with jax.named_scope("pair_arrives"):
        for c in pair_cp:
            c.wait_recv()
    chips = ntp // 2
    mine, came = l_send[side].reshape(chips, N), l_pair[...].reshape(chips, N)
    peak = jnp.maximum(mine, came)
    w_mine, w_came = jnp.exp(mine - peak), jnp.exp(came - peak)
    total = w_mine + w_came
    lses_v[...] = peak + jnp.log(total)
    xpad[0:chips, 0:N] = w_mine / total
    xpad[chips : 2 * chips, 0:N] = w_came / total
    cols = xpad[:, 0:N].T
    for k in range(chips):
        both = cols[0:xrows, k : k + 1] * x_send[side, k].astype(F32)
        both = both + cols[0:xrows, chips + k : chips + k + 1] * x_pair[k].astype(F32)
        xc_send[k] = both.astype(BF16)
        lc_send[k] = lses_v[k : k + 1, :]

    def x_copies(k):
        to = peer(2 * k)
        return (
            send(xc_send.at[to // 2], xc_recv.at[k], x_ss.at[k], x_rs.at[k], (r, to)),
            send(lc_send.at[to // 2], lc_recv.at[k], l_ss.at[k], l_rs.at[k], (r, to)),
        )

    def each_chip(act):
        def one(k, _):
            for c in x_copies(k):
                act(c)
            return 0

        lax.fori_loop(1, chips, one, 0)

    each_chip(lambda c: c.start())
    xc_recv[0] = xc_send[t // 2]
    lc_recv[0] = lc_send[t // 2]

    def place_page(n, _):
        fin_pool[n] = newp[tab[T_INV + n]]
        return 0

    lax.fori_loop(0, SLOTS, place_page, 0)
    outs = [pltpu.make_async_copy(fin_pool, pool_out, out_sem.at[0])]
    outs[0].start()

    with jax.named_scope("partials_arrive"):
        each_chip(lambda c: c.wait_recv())
    lses = lc_recv[...].reshape(chips, N)
    w = jnp.exp(lses - jnp.max(lses, axis=0, keepdims=True))
    w = w / jnp.sum(w, axis=0, keepdims=True)
    xpad[0:chips, 0:N] = w
    cols = xpad[:, 0:N].T
    total = jnp.zeros((xrows, HD), F32)
    for k in range(chips):
        total = total + cols[0:xrows, k : k + 1] * xc_recv[k].astype(F32)
    for s in range(STEPS):
        for h in range(share):
            attn_v[s, :, h * HD : (h + 1) * HD] = total[
                h * SI + s * ROWS : h * SI + (s + 1) * ROWS
            ].astype(BF16)
    outs.append(pltpu.make_async_copy(attn_v, attn_hbm, out_sem.at[1]))
    outs[1].start()

    for c in m_cp:
        c.wait_recv()
    for d in range(2):
        for k in range(MV):
            m_all[ROWS + d * MV + k] = m_recv[d, k]
    for i in range(ROWS):
        row = m_all[tab[T_ROW + i]]
        for s in range(STEPS):
            for m in range(CH // N):
                ybuf[s * ROWS + i : s * ROWS + i + 1, m * N : (m + 1) * N] = row[
                    s * (CH // N) + m : s * (CH // N) + m + 1
                ]
    for s in range(STEPS):
        mixer_v[s] = ybuf[s * ROWS : (s + 1) * ROWS].astype(BF16)
    outs.append(pltpu.make_async_copy(mixer_v, mixer_hbm, out_sem.at[2]))
    outs[2].start()

    with jax.named_scope("rows_arrive"):
        for c in b_cp:
            c.wait_recv()

    def place_row(n, _):
        i, j = n // HPD, n % HPD
        at = tab[T_ROW + i]
        away = jnp.maximum(at - ROWS, 0)
        mine = rowbuf[jnp.minimum(at, ROWS - 1), j]
        came = b_recv[away // MV, away % MV, j].astype(F32)
        fin_state[i, j] = jnp.where(at < ROWS, mine, came)
        return 0

    for i in range(ROWS):
        lax.fori_loop(i * HPD, (i + 1) * HPD, place_row, 0)
        outs.append(pltpu.make_async_copy(fin_state.at[i], state_out.at[i], out_sem.at[3 + i]))
        outs[3 + i].start()

    with jax.named_scope("all_sent"):
        for c in a_cp + p_cp + r_cp + c_cp + b_cp + m_cp + pair_cp:
            c.wait_send()
        each_peer(lambda k: s_copy(k).wait_send())
        each_chip(lambda c: c.wait_send())
        for c in outs:
            c.wait()


def hand_over(mixer, attn, state, pool, mixer_out, attn_out, state_out, pool_out, m_v, a_v, s_v, p_v, sem):
    pieces = []
    for src, mid, dst in ((state, s_v, state_out), (pool, p_v, pool_out)):
        size = src.shape[0] // PIECES
        for k in range(PIECES):
            part = pl.ds(k * size, size)
            pieces.append((src.at[part], mid.at[part], dst.at[part]))
    pieces += [(mixer, m_v, mixer_out), (attn, a_v, attn_out)]
    loads, stores = [], []
    for k, (src, mid, dst) in enumerate(pieces):
        loads.append(pltpu.make_async_copy(src, mid, sem.at[0, k]))
        stores.append(pltpu.make_async_copy(mid, dst, sem.at[1, k]))
    for c in loads:
        c.start()
    for load, store in zip(loads, stores):
        load.wait()
        store.start()
    for c in stores:
        c.wait()


def per_device(ntp, nreq, *arguments):
    (
        scan_state, decay_rate, step_bias, skip_gain, norm_gain, page_pool, old_table, new_table,
        request_source, head_source, context_lengths, mixer_input, mixer_gate, step_raw, state_maps,
        queries, new_entries,
    ) = arguments
    xrows = QH // ntp * SI
    anywhere = pl.BlockSpec(memory_space=pl.ANY)
    dma = pltpu.SemaphoreType.DMA
    scratch = [
        ((ROWS, HPD + 2 * HMV, P_SIZE, N), F32),
        ((2, HMV, ROWS, P_SIZE, N), BF16),
        ((2, HMV, ROWS, P_SIZE, N), BF16),
        ((ROWS, HPD, P_SIZE, N), F32),
        ((2, MV, HPD, P_SIZE, N), BF16),
        ((2, MV, HPD, P_SIZE, N), BF16),
        ((SLOTS, PAGE, KVW), BF16),
        ((2 * MV * PGS, PAGE, KVW), BF16),
        ((2 * MV * PGS, PAGE, KVW), BF16),
        ((SLOTS, PAGE, KVW), BF16),
        ((SLOTS, PAGE, KVW), BF16),
        ((ROWS, HPD, P_SIZE, N), F32),
        (norm_gain.shape, F32),
        (mixer_input.shape, BF16),
        (mixer_gate.shape, BF16),
        (state_maps.shape, BF16),
        (queries.shape, BF16),
        (new_entries.shape, BF16),
        ((2 * HPD, N), F32),
        ((2, 2 * HPD, N), F32),
        ((3 * HPD, N), F32),
        ((3 * HPD, N), F32),
        ((HPD, N), F32),
        ((HPD, N), F32),
        ((HPD, N), F32),
        ((HPD, N), F32),
        ((2, SI, CH), F32),
        ((ROWS, REC, CH), BF16),
        ((2, MV, REC, CH), BF16),
        ((2, MV, REC, CH), BF16),
        ((ROWS, REC, CH), F32),
        ((N, CH), F32),
        ((CH, N), F32),
        ((SI, QH * HD), F32),
        ((SI, KVW), F32),
        ((G, 2 * SI, N), F32),
        ((SI, HPD, N), F32),
        ((SI, HPD, P_SIZE, N), F32),
        ((CH, N), F32),
        ((1, CH), F32),
        ((1, CH), F32),
        ((STEPS, CH, N), F32),
        ((SI, CH), F32),
        ((QH, SLOTS * PAGE), F32),
        ((2, ntp // 2, xrows, HD), BF16),
        ((2, ntp // 2, 1, N), F32),
        ((ntp // 2, xrows, HD), BF16),
        ((ntp // 2, 1, N), F32),
        ((ntp // 2, xrows, HD), BF16),
        ((ntp // 2, xrows, HD), BF16),
        ((ntp // 2, 1, N), F32),
        ((ntp // 2, 1, N), F32),
        ((ntp // 2, N), F32),
        ((1, N), F32),
        ((ntp, 1, N), F32),
        ((2, MV, SI, N), F32),
        ((2, MV, SI, N), F32),
        ((ROWS + 2 * MV, SI, N), F32),
        ((STEPS, ROWS, CH), BF16),
        ((STEPS, ROWS, CH), BF16),
        (step_raw.shape, F32),
    ]
    results = pl.pallas_call(
        lambda *refs: kernel(ntp, nreq, *refs),
        out_shape=(
            jax.ShapeDtypeStruct((STEPS, ROWS, CH), BF16),
            jax.ShapeDtypeStruct((STEPS, ROWS, CH), BF16),
            jax.ShapeDtypeStruct(scan_state.shape, F32),
            jax.ShapeDtypeStruct(page_pool.shape, BF16),
        ),
        in_specs=[pl.BlockSpec(memory_space=pltpu.HBM)] * 17,
        out_specs=(anywhere,) * 4,
        scratch_shapes=[pltpu.VMEM(shape, dtype) for shape, dtype in scratch]
        + [
            *[pltpu.SMEM((HPD,), F32) for _ in range(3)],
            *[pltpu.SMEM((ROWS, 1, PGS), I32) for _ in range(2)],
            *[pltpu.SMEM(ints.shape, I32) for ints in (request_source, head_source, context_lengths)],
            pltpu.SMEM((128,), I32),
            dma((9,)),
            dma((8,)),
            *[dma((2,)) for _ in range(14)],
            *[dma((ntp,)) for _ in range(6)],
            dma((3 + ROWS,)),
        ],
        compiler_params=pltpu.CompilerParams(
            collective_id=0, has_side_effects=True, vmem_limit_bytes=63 * 2**20
        ),
        name="decode",
    )(
        scan_state, norm_gain, page_pool, mixer_input, mixer_gate, state_maps, queries, new_entries,
        step_raw, decay_rate, step_bias, skip_gain, old_table.transpose(0, 2, 1), new_table.transpose(0, 2, 1),
        request_source, head_source, context_lengths,
    )
    return pl.pallas_call(
        hand_over,
        out_shape=[jax.ShapeDtypeStruct(x.shape, x.dtype) for x in results],
        in_specs=[anywhere] * 4,
        out_specs=[anywhere] * 4,
        scratch_shapes=[pltpu.VMEM(x.shape, x.dtype) for x in results] + [dma((2, 2 + 2 * PIECES))],
        compiler_params=pltpu.CompilerParams(vmem_limit_bytes=63 * 2**20),
        name="hand_over",
    )(*results)


def solution(mesh):
    ntp, nreq = mesh.shape["tp"], mesh.shape["req"]
    return jax.shard_map(
        lambda *arguments: per_device(ntp, nreq, *arguments),
        mesh=mesh,
        in_specs=(
            P("req", "tp", None, None),
            P("tp"),
            P("tp"),
            P("tp"),
            P("tp", None),
            P(("req", "tp"), None, None),
            P("req", None, "tp"),
            P("req", None, "tp"),
            P(),
            P(),
            P(),
            P(None, "req", "tp"),
            P(None, "req", "tp"),
            P(None, "req", "tp"),
            P(None, "req", None, None),
            P(None, "req", None),
            P(None, "req", None),
        ),
        out_specs=(
            P(None, "req", "tp"),
            P(None, "req", "tp"),
            P("req", "tp", None, None),
            P(("req", "tp"), None, None),
        ),
        check_vma=False,
    )
```

```python
import math

import jax
import jax.numpy as jnp
from jax import lax
from jax.experimental import pallas as pl
from jax.experimental.pallas import tpu as pltpu
from jax.sharding import PartitionSpec as P

MESH = pl.DeviceIdType.MESH
HIGH = lax.Precision.HIGHEST
F32 = jnp.float32
BF16 = jnp.bfloat16
I32 = jnp.int32

P_SIZE = 64
N = 128
G = 8
QH = 64
KVH = 8
HD = 128
PAGE = 16
STEPS = 2
ROWS = 4
PGS = 4
MV = 2
HPD = 8
HMV = 4
HEADS_PER_GROUP = 16
GROUP_CHANNELS = 1024
KVW = 2048
SLOTS = ROWS * PGS
SI = STEPS * ROWS
CH = HPD * P_SIZE
NEG = -1e30
EPSILON = 1e-05

T_AR, T_AL, T_HEAD, T_BR, T_BL, T_ROW = 0, 4, 8, 16, 18, 20
T_OWNPG, T_RECVPG, T_ISOWN, T_INV, T_GROUP, T_LEN, T_PAR = 24, 40, 56, 60, 76, 84, 88
T_RR, T_RL, T_REC = 96, 98, 100
PIECES = 4
REC, REC_X, REC_GATE, REC_MAPS, REC_RAW = 16, 0, 2, 4, 12


def dot_nt(a, b, precision=None):
    return lax.dot_general(
        a, b, (((1,), (1,)), ((), ())), precision=precision, preferred_element_type=F32
    )


def choose(source, base, count, block, most):
    picks = [jnp.int32(0)] * most
    seen = jnp.int32(0)
    for i in range(count):
        v = source[base + i]
        hit = v // count == block
        for k in range(most):
            picks[k] = jnp.where(hit & (seen == k), v - block * count, picks[k])
        seen = seen + hit.astype(I32)
    return picks


def choose_slots(source, base, count, block, most):
    picks = [jnp.int32(0)] * most
    seen = jnp.int32(0)
    for i in range(count):
        hit = source[base + i] // count == block
        for k in range(most):
            picks[k] = jnp.where(hit & (seen == k), i, picks[k])
        seen = seen + hit.astype(I32)
    return picks


def kernel(ntp, nreq, *refs):
    (
        state_hbm, gain_hbm, pool_hbm, x_hbm, gate_hbm, maps_hbm, q_hbm, entry_hbm,
        raw_hbm, rate_h, bias_h, skip_h, old_h, new_h, rsrc_h, hsrc_h, ctx_h,
        mixer_v, attn_v, fin_state, fin_pool,
        own, a_send, a_recv, rowbuf, b_send, b_recv, pool_v, c_send, c_recv, newp,
        gain_in, x_in, gate_in, maps_in, q_in, entry_in,
        p_own, p_recv, p_gain, p_scal, slot_scal, dt_v, decay_v, raw_t,
        xf, rec, r_send, r_recv, recf, xpad, x_t, qf, ef, maps_g, c_rows, outer, member, skip_row, gain_row,
        stash, ybuf, vis, x_send, l_send, x_pair, l_pair, xc_send, xc_recv, lc_send, lc_recv, lses_v, s_send, s_recv, m_send, m_recv, m_all,
        raw_in,
        rate_s, bias_s, skip_s, old_s, new_s, rsrc, hsrc, ctx, tab,
        in_sem, scalar_sem, r_ss, r_rs, m_ss, m_rs, a_ss, a_rs, p_ss, p_rs, b_ss, b_rs, c_ss, c_rs, pair_ss, pair_rs, x_ss, x_rs, l_ss, l_rs, s_ss, s_rs,
    ) = refs
    share = QH // ntp
    xrows = share * SI
    t = lax.axis_index("tp")
    r = lax.axis_index("req")
    t_right, t_left = lax.rem(t + 1, ntp), lax.rem(t + ntp - 1, ntp)
    r_right, r_left = lax.rem(r + 1, nreq), lax.rem(r + nreq - 1, nreq)
    dev = {"tr": (r, t_right), "tl": (r, t_left), "rr": (r_right, t), "rl": (r_left, t)}

    scalars = [
        pltpu.make_async_copy(src, dst, scalar_sem.at[k])
        for k, (src, dst) in enumerate(
            (
                (hsrc_h, hsrc), (rsrc_h, rsrc), (old_h, old_s), (ctx_h, ctx), (new_h, new_s),
                (rate_h, rate_s), (bias_h, bias_s), (skip_h, skip_s),
            )
        )
    ]
    loads = [
        pltpu.make_async_copy(state_hbm, own.at[:, pl.ds(0, HPD)], in_sem.at[0]),
        pltpu.make_async_copy(pool_hbm, pool_v, in_sem.at[1]),
        pltpu.make_async_copy(gain_hbm, gain_in, in_sem.at[2]),
        pltpu.make_async_copy(x_hbm, x_in, in_sem.at[3]),
        pltpu.make_async_copy(gate_hbm, gate_in, in_sem.at[4]),
        pltpu.make_async_copy(maps_hbm, maps_in, in_sem.at[5]),
        pltpu.make_async_copy(q_hbm, q_in, in_sem.at[6]),
        pltpu.make_async_copy(entry_hbm, entry_in, in_sem.at[7]),
        pltpu.make_async_copy(raw_hbm, raw_in, in_sem.at[8]),
    ]
    for c in scalars[:1] + loads[:1]:
        c.start()

    barrier = pltpu.get_barrier_semaphore()
    for name in ("rr", "rl"):
        pl.semaphore_signal(barrier, inc=1, device_id=dev[name], device_id_type=MESH)

    def peer(k):
        core, y_hi = (t + k) % 2, (t // 2 + k // 2) % 2
        return (t // 4 + k // 4) % (ntp // 4) * 4 + y_hi * 2 + core

    def each_peer(act):
        def far(n, _):
            act(n // 2 * 4 + 2 + n % 2)
            return 0

        def near(n, _):
            act(n // 2 * 4 + n % 2)
            return 0

        lax.fori_loop(0, ntp // 2, far, 0)
        lax.fori_loop(1, ntp // 2, near, 0)

    def greet(k):
        pl.semaphore_signal(barrier, inc=1, device_id=(r, peer(k)), device_id_type=MESH)

    each_peer(greet)

    for c in scalars[1:] + loads[1:]:
        c.start()

    with jax.named_scope("scalars"):
        scalars[0].wait()
    for k, v in enumerate(choose(hsrc, t_right * HPD, HPD, t, HMV)):
        tab[T_AR + k] = v
    for k, v in enumerate(choose(hsrc, t_left * HPD, HPD, t, HMV)):
        tab[T_AL + k] = v

    loads[0].wait()

    def pack_a(n, _):
        d, k, q = n // (HMV * ROWS), (n // ROWS) % HMV, n % ROWS
        a_send[d, k, q] = own[q, tab[T_AR + d * HMV + k]].astype(BF16)
        return 0

    lax.fori_loop(0, 2 * HMV * ROWS, pack_a, 0)

    with jax.named_scope("entry_barrier"):
        pl.semaphore_wait(barrier, ntp + 1)

    def send(src, dst, ss, rs, to):
        return pltpu.make_async_remote_copy(
            src_ref=src, dst_ref=dst, send_sem=ss, recv_sem=rs, device_id=to, device_id_type=MESH
        )

    a_cp = [
        send(a_send.at[d], a_recv.at[d], a_ss.at[d], a_rs.at[d], dev[("tr", "tl")[d]])
        for d in range(2)
    ]
    for c in a_cp:
        c.start()

    for c in scalars[1:]:
        c.wait()
    loads[2].wait()
    sub = lax.broadcasted_iota(I32, (HPD, N), 0)
    lane = lax.broadcasted_iota(I32, (HPD, N), 1)
    p_own[0:HPD, 0:P_SIZE] = gain_in[...]
    wide = p_own[0:HPD, :]
    p_own[0:HPD, :] = jnp.where(lane < P_SIZE, wide, pltpu.roll(wide, P_SIZE, 1))
    scal = jnp.zeros((HPD, N), F32)
    for h in range(HPD):
        for place, ref in enumerate((bias_s, rate_s, skip_s)):
            scal = jnp.where((sub == h) & (lane == place), ref[h], scal)
    p_own[HPD : 2 * HPD, :] = scal
    p_cp = [
        send(p_own, p_recv.at[d], p_ss.at[d], p_rs.at[d], dev[("tr", "tl")[d]]) for d in range(2)
    ]
    for c in p_cp:
        c.start()

    for k, v in enumerate(choose(rsrc, r_right * ROWS, ROWS, r, MV)):
        tab[T_BR + k] = v
    for k, v in enumerate(choose(rsrc, r_left * ROWS, ROWS, r, MV)):
        tab[T_BL + k] = v
    for k, v in enumerate(choose_slots(rsrc, r * ROWS, ROWS, r_right, MV)):
        tab[T_RR + k] = v
    for k, v in enumerate(choose_slots(rsrc, r * ROWS, ROWS, r_left, MV)):
        tab[T_RL + k] = v
    records = [jnp.int32(0)] * ROWS
    for block, base in ((r_left, ROWS), (r, 0), (r_right, ROWS + MV)):
        rank = jnp.int32(0)
        for i in range(ROWS):
            v = rsrc[block * ROWS + i]
            hit = v // ROWS == r
            where = jnp.clip(rank, 0, MV - 1) + base if base else i
            for q in range(ROWS):
                records[q] = jnp.where(hit & (v - r * ROWS == q), where, records[q])
            rank = rank + hit.astype(I32)
    for q in range(ROWS):
        tab[T_REC + q] = records[q]
    lefts, rights = jnp.int32(0), jnp.int32(0)
    for j in range(HPD):
        v = hsrc[t * HPD + j]
        far = v // HPD - t
        place = jnp.where(far == 0, v - t * HPD, jnp.where(far < 0, HPD + lefts, HPD + HMV + rights))
        tab[T_HEAD + j] = jnp.clip(place, 0, HPD + 2 * HMV - 1)
        tab[T_PAR + j] = jnp.clip(v - t * HPD + HPD, 0, 3 * HPD - 1)
        tab[T_GROUP + j] = v // HEADS_PER_GROUP
        lefts = lefts + (far < 0).astype(I32)
        rights = rights + (far > 0).astype(I32)
    lefts, rights = jnp.int32(0), jnp.int32(0)
    for i in range(ROWS):
        v = rsrc[r * ROWS + i]
        far = v // ROWS - r
        here = jnp.where(far == 0, v - r * ROWS, 0)
        away = jnp.where(far < 0, lefts, MV + rights)
        away = jnp.clip(jnp.where(far == 0, 0, away), 0, 2 * MV - 1)
        tab[T_ROW + i] = jnp.where(far == 0, here, ROWS + away)
        tab[T_ISOWN + i] = (far == 0).astype(I32)
        tab[T_LEN + i] = ctx[v]
        for g in range(PGS):
            tab[T_OWNPG + i * PGS + g] = old_s[here, 0, g]
            tab[T_RECVPG + i * PGS + g] = away * PGS + g
        lefts = lefts + (far < 0).astype(I32)
        rights = rights + (far > 0).astype(I32)

    for c in loads[3:6] + loads[8:9]:
        c.wait()
    xpad[...] = jnp.zeros_like(xpad)
    rec[...] = jnp.zeros_like(rec)
    for s in range(STEPS):
        xpad[s * ROWS : (s + 1) * ROWS, 0:HPD] = raw_in[s]
        xf[0, s * ROWS : (s + 1) * ROWS, :] = x_in[s].astype(F32)
        xf[1, s * ROWS : (s + 1) * ROWS, :] = gate_in[s].astype(F32)
    for i in range(ROWS):
        parts = [xf[0, k : k + 1, :] for k in (i, ROWS + i)]
        parts += [xf[1, k : k + 1, :] for k in (i, ROWS + i)]
        for s in range(STEPS):
            maps = maps_in[s, i].astype(F32)
            for bc in range(2):
                parts += [maps[bc : bc + 1, h * CH : (h + 1) * CH] for h in range(2)]
        raws = jnp.concatenate([xpad[i : i + 1, 0:N], xpad[ROWS + i : ROWS + i + 1, 0:N]], axis=1)
        rest = jnp.concatenate([raws, jnp.zeros((1, CH - 2 * N), F32)], axis=1)
        for _ in range(3):
            top = rest.astype(BF16).astype(F32)
            parts.append(top)
            rest = rest - top
        parts.append(rest)
        rec[i] = jnp.concatenate(parts, axis=0).astype(BF16)
    for d in range(2):
        for k in range(MV):
            r_send[d, k] = rec[tab[T_RR + d * MV + k]]

    r_cp = [
        send(r_send.at[d], r_recv.at[d], r_ss.at[d], r_rs.at[d], dev[("rr", "rl")[d]])
        for d in range(2)
    ]
    for c in r_cp:
        c.start()

    loads[1].wait()

    def pack_c(n, _):
        d, k, g = n // (MV * PGS), (n // PGS) % MV, n % PGS
        c_send[n] = pool_v[old_s[tab[T_BR + d * MV + k], 0, g]]
        return 0

    lax.fori_loop(0, 2 * MV * PGS, pack_c, 0)

    c_cp = []
    for d in range(2):
        part = pl.ds(d * MV * PGS, MV * PGS)
        c_cp.append(
            send(c_send.at[part], c_recv.at[part], c_ss.at[d], c_rs.at[d], dev[("rr", "rl")[d]])
        )
    for c in c_cp:
        c.start()

    for i in range(SLOTS):
        found = jnp.int32(0)
        for e in range(SLOTS):
            found = jnp.where(new_s[e // PGS, 0, e % PGS] == i, e, found)
        tab[T_INV + i] = found
    for c in loads[6:8]:
        c.wait()
    for s in range(STEPS):
        part = slice(s * ROWS, (s + 1) * ROWS)
        qf[part, :] = q_in[s].astype(F32)
        ef[part, :] = entry_in[s].astype(F32)

    rowid = lax.broadcasted_iota(I32, (QH, ROWS * PGS * PAGE), 0)
    colid = lax.broadcasted_iota(I32, (QH, ROWS * PGS * PAGE), 1)
    row_i = rowid % ROWS
    limit = (rowid // ROWS) % STEPS
    for i in range(ROWS):
        limit = limit + jnp.where(row_i == i, tab[T_LEN + i], 0)
    place = ((colid // PAGE) % PGS * ntp + t) * PAGE + colid % PAGE
    seen = (row_i == colid // (PGS * PAGE)) & (place <= limit)
    vis[...] = jnp.where(seen, 1.0, 0.0)

    with jax.named_scope("params_arrive"):
        for c in p_cp + r_cp:
            c.wait_recv()
    for part, buf in enumerate((p_gain, p_scal)):
        rows = slice(part * HPD, (part + 1) * HPD)
        buf[0:HPD, :] = p_recv[0, rows, :]
        buf[HPD : 2 * HPD, :] = p_own[rows, :]
        buf[2 * HPD : 3 * HPD, :] = p_recv[1, rows, :]
    for j in range(HPD):
        slot_scal[j : j + 1, :] = p_scal[pl.ds(tab[T_PAR + j], 1), :]
    bias, rate, skip = (slot_scal[:, k : k + 1] for k in range(3))
    for q in range(ROWS):
        at = tab[T_REC + q]
        mine = rec[jnp.minimum(at, ROWS - 1)].astype(F32)
        away = jnp.maximum(at - ROWS, 0)
        came = r_recv[away // MV, away % MV].astype(F32)
        recf[q] = jnp.where(at < ROWS, mine, came)
    for q in range(ROWS):
        raws = recf[q, REC_RAW : REC_RAW + 1, :]
        for k in range(1, 3):
            raws = raws + recf[q, REC_RAW + k : REC_RAW + k + 1, :]
        for s in range(STEPS):
            k = s * ROWS + q
            xf[0, k : k + 1, :] = recf[q, REC_X + s : REC_X + s + 1, :]
            xf[1, k : k + 1, :] = recf[q, REC_GATE + s : REC_GATE + s + 1, :]
            xpad[k : k + 1, 0:N] = raws[:, s * N : (s + 1) * N]
            for bc in range(2):
                for g in range(G):
                    row = REC_MAPS + (s * 2 + bc) * 2 + g // (G // 2)
                    lanes = slice(g % (G // 2) * N, (g % (G // 2) + 1) * N)
                    maps_g[g, 2 * k + bc : 2 * k + bc + 1, :] = recf[q, row : row + 1, lanes]
    raw_t[...] = xpad[:, 0:N].T[0:HPD, :]
    xpad[0:SI, :] = xf[0]
    for m in range(CH // N):
        x_t[m * N : (m + 1) * N, :] = xpad[:, m * N : (m + 1) * N].T
    v = raw_t[...] + bias
    dt = jnp.maximum(v, 0.0) + jnp.log1p(jnp.exp(-jnp.abs(v)))
    dt_v[...] = dt
    decay_v[...] = jnp.exp(-rate * dt)
    lane1 = lax.broadcasted_iota(I32, (1, N), 1)
    for m in range(CH // N):
        lanes = slice(m * N, (m + 1) * N)
        first = p_gain[pl.ds(tab[T_PAR + 2 * m], 1), :]
        second = p_gain[pl.ds(tab[T_PAR + 2 * m + 1], 1), :]
        gain_row[:, lanes] = jnp.where(lane1 < P_SIZE, first, second)
        skip_row[:, lanes] = jnp.where(
            lane1 < P_SIZE,
            jnp.broadcast_to(skip[2 * m : 2 * m + 1], (1, N)),
            jnp.broadcast_to(skip[2 * m + 1 : 2 * m + 2], (1, N)),
        )
    lane64 = lax.broadcasted_iota(I32, (P_SIZE, N), 1)

    def prepare(j, _):
        group = tab[T_GROUP + j]
        member[pl.ds(pl.multiple_of(j * P_SIZE, P_SIZE), P_SIZE), :] = jnp.where(
            lane64 % G == group, 1.0, 0.0
        )
        both = maps_g[group]
        dts = dt_v[pl.ds(j, 1), :]
        cols = x_t[pl.ds(pl.multiple_of(j * P_SIZE, P_SIZE), P_SIZE), :]
        for k in range(SI):
            outer[k, j] = cols[:, k : k + 1] * (dts[:, k : k + 1] * both[2 * k : 2 * k + 1, :])
            c_rows[k, pl.ds(j, 1), :] = both[2 * k + 1 : 2 * k + 2, :]
        return 0

    lax.fori_loop(0, HPD, prepare, 0)

    with jax.named_scope("heads_arrive"):
        for c in a_cp:
            c.wait_recv()

    def take_a(n, _):
        k, q = n // ROWS, n % ROWS
        own[q, HPD + k] = a_recv[k // HMV, k % HMV, q].astype(F32)
        return 0

    lax.fori_loop(0, 2 * HMV * ROWS, take_a, 0)

    diagonal = lax.broadcasted_iota(I32, (HPD, CH), 0) == (
        lax.broadcasted_iota(I32, (HPD, CH), 1) // P_SIZE
    )
    for i in range(ROWS):

        def step(j, _):
            now = own[i, tab[T_HEAD + j]]
            fade = decay_v[pl.ds(j, 1), :]
            for s in range(STEPS):
                k = s * ROWS + i
                now = fade[:, k : k + 1] * now + outer[k, j]
                stash[s, pl.ds(pl.multiple_of(j * P_SIZE, P_SIZE), P_SIZE), :] = now
            rowbuf[i, j] = now
            return 0

        lax.fori_loop(0, HPD, step, 0)
        for s in range(STEPS):
            k = s * ROWS + i
            now = stash[s]
            top = now.astype(BF16)
            low = (now - top.astype(F32)).astype(BF16)
            c8 = c_rows[k].astype(BF16)
            y = dot_nt(c8, top) + dot_nt(c8, low)
            ybuf[k : k + 1, :] = jnp.sum(jnp.where(diagonal, y, 0.0), axis=0, keepdims=True)

    gate = xf[1]
    gated = (ybuf[...] + skip_row[...] * xf[0]) * (gate / (1.0 + jnp.exp(-gate)))
    packed = sub == lane // G
    squares = jnp.dot(gated * gated, member[...], precision=HIGH, preferred_element_type=F32)
    s_send[...] = jnp.sum(jnp.where(packed, squares, 0.0), axis=0, keepdims=True)

    def s_copy(k):
        return send(s_send, s_recv.at[k], s_ss.at[k], s_rs.at[k], (r, peer(k)))

    each_peer(lambda k: s_copy(k).start())
    s_recv[0] = s_send[...]

    def pack_b(n, _):
        d, k, j = n // (MV * HPD), (n // HPD) % MV, n % HPD
        b_send[d, k, j] = rowbuf[tab[T_BR + d * MV + k], j].astype(BF16)
        return 0

    lax.fori_loop(0, 2 * MV * HPD, pack_b, 0)
    b_cp = [
        send(b_send.at[d], b_recv.at[d], b_ss.at[d], b_rs.at[d], dev[("rr", "rl")[d]])
        for d in range(2)
    ]

    for c in b_cp:
        c.start()

    with jax.named_scope("pages_arrive"):
        for c in c_cp:
            c.wait_recv()

    offset = lax.broadcasted_iota(I32, (PAGE, KVW), 0)

    def take_page(n, _):
        i, g = n // PGS, n % PGS
        mine = pool_v[tab[T_OWNPG + n]].astype(F32)
        came = c_recv[tab[T_RECVPG + n]].astype(F32)
        page = jnp.where(tab[T_ISOWN + i] == 1, mine, came)
        for s in range(STEPS):
            position = tab[T_LEN + i] + s
            logical = position // PAGE
            hit = (logical % ntp == t) & (logical // ntp == g)
            at = jnp.where(hit, position % PAGE, -1)
            page = jnp.where(offset == at, ef[pl.ds(s * ROWS + i, 1), :], page)
        newp[n] = page.astype(BF16)
        return 0

    lax.fori_loop(0, SLOTS, take_page, 0)

    eye = lax.broadcasted_iota(I32, (xrows, N), 0) == lax.broadcasted_iota(I32, (xrows, N), 1)
    shown = vis[...] > 0.5
    per = QH // KVH
    for g in range(KVH):
        q = jnp.concatenate(
            [qf[:, (g * per + h) * HD : (g * per + h + 1) * HD] for h in range(per)], axis=0
        ).astype(BF16)
        keys = newp[:, :, g * HD : (g + 1) * HD].reshape(SLOTS * PAGE, HD)
        values = newp[:, :, (KVH + g) * HD : (KVH + g + 1) * HD].reshape(SLOTS * PAGE, HD)
        scores = jnp.where(shown, dot_nt(q, keys) * (1.0 / math.sqrt(HD)), NEG)
        peak = jnp.max(scores, axis=1, keepdims=True)
        weights = jnp.where(shown, jnp.exp(scores - peak), 0.0).astype(BF16)
        total = jnp.sum(weights.astype(F32), axis=1, keepdims=True)
        part = jnp.dot(weights, values, preferred_element_type=F32)
        safe = jnp.maximum(total, 1e-30)
        part = (part / safe).astype(BF16)
        lse = jnp.where(total > 0.0, peak + jnp.log(safe), NEG)
        for e in range(per // share):
            rows = slice(e * xrows, (e + 1) * xrows)
            dest = g * (per // share) + e
            x_send[dest % 2, dest // 2] = part[rows]
            l_send[dest % 2, dest // 2] = jnp.sum(
                jnp.where(eye, lse[rows], 0.0), axis=0, keepdims=True
            )

    side = t % 2
    other = (r, t + 1 - 2 * side)
    pair_cp = [
        send(x_send.at[1 - side], x_pair, pair_ss.at[0], pair_rs.at[0], other),
        send(l_send.at[1 - side], l_pair, pair_ss.at[1], pair_rs.at[1], other),
    ]
    for c in pair_cp:
        c.start()

    with jax.named_scope("squares_arrive"):
        each_peer(lambda k: s_copy(k).wait_recv())
    squares = jnp.sum(s_recv[...], axis=0)
    scale = jnp.where(packed, lax.rsqrt(squares * (1.0 / GROUP_CHANNELS) + EPSILON), 0.0)
    mixed = gated * dot_nt(scale, member[...], HIGH) * gain_row[...]
    for q in range(ROWS):
        for s in range(STEPS):
            for m in range(CH // N):
                k = s * ROWS + q
                m_all[q, s * (CH // N) + m : s * (CH // N) + m + 1, :] = mixed[
                    k : k + 1, m * N : (m + 1) * N
                ]
    for d in range(2):
        for k in range(MV):
            m_send[d, k] = m_all[tab[T_BR + d * MV + k]]
    m_cp = [
        send(m_send.at[d], m_recv.at[d], m_ss.at[d], m_rs.at[d], dev[("rr", "rl")[d]])
        for d in range(2)
    ]
    for c in m_cp:
        c.start()

    with jax.named_scope("pair_arrives"):
        for c in pair_cp:
            c.wait_recv()
    chips = ntp // 2
    mine, came = l_send[side].reshape(chips, N), l_pair[...].reshape(chips, N)
    peak = jnp.maximum(mine, came)
    w_mine, w_came = jnp.exp(mine - peak), jnp.exp(came - peak)
    total = w_mine + w_came
    lses_v[...] = peak + jnp.log(total)
    xpad[0:chips, 0:N] = w_mine / total
    xpad[chips : 2 * chips, 0:N] = w_came / total
    cols = xpad[:, 0:N].T
    for k in range(chips):
        both = cols[0:xrows, k : k + 1] * x_send[side, k].astype(F32)
        both = both + cols[0:xrows, chips + k : chips + k + 1] * x_pair[k].astype(F32)
        xc_send[k] = both.astype(BF16)
        lc_send[k] = lses_v[k : k + 1, :]

    def x_copies(k):
        to = peer(2 * k)
        return (
            send(xc_send.at[to // 2], xc_recv.at[k], x_ss.at[k], x_rs.at[k], (r, to)),
            send(lc_send.at[to // 2], lc_recv.at[k], l_ss.at[k], l_rs.at[k], (r, to)),
        )

    def each_chip(act):
        def one(k, _):
            for c in x_copies(k):
                act(c)
            return 0

        lax.fori_loop(1, chips, one, 0)

    each_chip(lambda c: c.start())
    xc_recv[0] = xc_send[t // 2]
    lc_recv[0] = lc_send[t // 2]

    def place_page(n, _):
        fin_pool[n] = newp[tab[T_INV + n]]
        return 0

    lax.fori_loop(0, SLOTS, place_page, 0)

    with jax.named_scope("partials_arrive"):
        each_chip(lambda c: c.wait_recv())
    lses = lc_recv[...].reshape(chips, N)
    w = jnp.exp(lses - jnp.max(lses, axis=0, keepdims=True))
    w = w / jnp.sum(w, axis=0, keepdims=True)
    xpad[0:chips, 0:N] = w
    cols = xpad[:, 0:N].T
    total = jnp.zeros((xrows, HD), F32)
    for k in range(chips):
        total = total + cols[0:xrows, k : k + 1] * xc_recv[k].astype(F32)
    for s in range(STEPS):
        for h in range(share):
            attn_v[s, :, h * HD : (h + 1) * HD] = total[
                h * SI + s * ROWS : h * SI + (s + 1) * ROWS
            ].astype(BF16)

    for c in m_cp:
        c.wait_recv()
    for d in range(2):
        for k in range(MV):
            m_all[ROWS + d * MV + k] = m_recv[d, k]
    for i in range(ROWS):
        row = m_all[tab[T_ROW + i]]
        for s in range(STEPS):
            for m in range(CH // N):
                ybuf[s * ROWS + i : s * ROWS + i + 1, m * N : (m + 1) * N] = row[
                    s * (CH // N) + m : s * (CH // N) + m + 1
                ]
    for s in range(STEPS):
        mixer_v[s] = ybuf[s * ROWS : (s + 1) * ROWS].astype(BF16)

    with jax.named_scope("rows_arrive"):
        for c in b_cp:
            c.wait_recv()

    def place_row(n, _):
        i, j = n // HPD, n % HPD
        at = tab[T_ROW + i]
        away = jnp.maximum(at - ROWS, 0)
        mine = rowbuf[jnp.minimum(at, ROWS - 1), j]
        came = b_recv[away // MV, away % MV, j].astype(F32)
        fin_state[i, j] = jnp.where(at < ROWS, mine, came)
        return 0

    lax.fori_loop(0, ROWS * HPD, place_row, 0)

    with jax.named_scope("all_sent"):
        for c in a_cp + p_cp + r_cp + c_cp + b_cp + m_cp + pair_cp:
            c.wait_send()
        each_peer(lambda k: s_copy(k).wait_send())
        each_chip(lambda c: c.wait_send())


def hand_over(mixer, attn, state, pool, mixer_out, attn_out, state_out, pool_out, sem):
    pieces = [(mixer, mixer_out), (attn, attn_out)]
    for src, dst in ((state, state_out), (pool, pool_out)):
        size = src.shape[0] // PIECES
        for k in range(PIECES):
            part = pl.ds(k * size, size)
            pieces.append((src.at[part], dst.at[part]))
    copies = [pltpu.make_async_copy(a, b, sem.at[k]) for k, (a, b) in enumerate(pieces)]
    for c in copies:
        c.start()
    for c in copies:
        c.wait()


def per_device(ntp, nreq, *arguments):
    (
        scan_state, decay_rate, step_bias, skip_gain, norm_gain, page_pool, old_table, new_table,
        request_source, head_source, context_lengths, mixer_input, mixer_gate, step_raw, state_maps,
        queries, new_entries,
    ) = arguments
    xrows = QH // ntp * SI
    anywhere = pl.BlockSpec(memory_space=pl.ANY)
    dma = pltpu.SemaphoreType.DMA
    scratch = [
        ((ROWS, HPD + 2 * HMV, P_SIZE, N), F32),
        ((2, HMV, ROWS, P_SIZE, N), BF16),
        ((2, HMV, ROWS, P_SIZE, N), BF16),
        ((ROWS, HPD, P_SIZE, N), F32),
        ((2, MV, HPD, P_SIZE, N), BF16),
        ((2, MV, HPD, P_SIZE, N), BF16),
        ((SLOTS, PAGE, KVW), BF16),
        ((2 * MV * PGS, PAGE, KVW), BF16),
        ((2 * MV * PGS, PAGE, KVW), BF16),
        ((SLOTS, PAGE, KVW), BF16),
        (norm_gain.shape, F32),
        (mixer_input.shape, BF16),
        (mixer_gate.shape, BF16),
        (state_maps.shape, BF16),
        (queries.shape, BF16),
        (new_entries.shape, BF16),
        ((2 * HPD, N), F32),
        ((2, 2 * HPD, N), F32),
        ((3 * HPD, N), F32),
        ((3 * HPD, N), F32),
        ((HPD, N), F32),
        ((HPD, N), F32),
        ((HPD, N), F32),
        ((HPD, N), F32),
        ((2, SI, CH), F32),
        ((ROWS, REC, CH), BF16),
        ((2, MV, REC, CH), BF16),
        ((2, MV, REC, CH), BF16),
        ((ROWS, REC, CH), F32),
        ((N, CH), F32),
        ((CH, N), F32),
        ((SI, QH * HD), F32),
        ((SI, KVW), F32),
        ((G, 2 * SI, N), F32),
        ((SI, HPD, N), F32),
        ((SI, HPD, P_SIZE, N), F32),
        ((CH, N), F32),
        ((1, CH), F32),
        ((1, CH), F32),
        ((STEPS, CH, N), F32),
        ((SI, CH), F32),
        ((QH, SLOTS * PAGE), F32),
        ((2, ntp // 2, xrows, HD), BF16),
        ((2, ntp // 2, 1, N), F32),
        ((ntp // 2, xrows, HD), BF16),
        ((ntp // 2, 1, N), F32),
        ((ntp // 2, xrows, HD), BF16),
        ((ntp // 2, xrows, HD), BF16),
        ((ntp // 2, 1, N), F32),
        ((ntp // 2, 1, N), F32),
        ((ntp // 2, N), F32),
        ((1, N), F32),
        ((ntp, 1, N), F32),
        ((2, MV, SI, N), F32),
        ((2, MV, SI, N), F32),
        ((ROWS + 2 * MV, SI, N), F32),
        (step_raw.shape, F32),
    ]
    results = pl.pallas_call(
        lambda *refs: kernel(ntp, nreq, *refs),
        out_shape=(
            pltpu.VMEM((STEPS, ROWS, CH), BF16),
            pltpu.VMEM((STEPS, ROWS, CH), BF16),
            pltpu.VMEM(scan_state.shape, F32),
            pltpu.VMEM(page_pool.shape, BF16),
        ),
        in_specs=[pl.BlockSpec(memory_space=pltpu.HBM)] * 17,
        out_specs=(pl.BlockSpec(memory_space=pltpu.VMEM),) * 4,
        scratch_shapes=[pltpu.VMEM(shape, dtype) for shape, dtype in scratch]
        + [
            *[pltpu.SMEM((HPD,), F32) for _ in range(3)],
            *[pltpu.SMEM((ROWS, 1, PGS), I32) for _ in range(2)],
            *[pltpu.SMEM(ints.shape, I32) for ints in (request_source, head_source, context_lengths)],
            pltpu.SMEM((128,), I32),
            dma((9,)),
            dma((8,)),
            *[dma((2,)) for _ in range(14)],
            *[dma((ntp,)) for _ in range(6)],
        ],
        compiler_params=pltpu.CompilerParams(
            collective_id=0, has_side_effects=True, vmem_limit_bytes=60 * 2**20
        ),
        name="decode",
    )(
        scan_state, norm_gain, page_pool, mixer_input, mixer_gate, state_maps, queries, new_entries,
        step_raw, decay_rate, step_bias, skip_gain, old_table.transpose(0, 2, 1), new_table.transpose(0, 2, 1),
        request_source, head_source, context_lengths,
    )
    return pl.pallas_call(
        hand_over,
        out_shape=[jax.ShapeDtypeStruct(x.shape, x.dtype) for x in results],
        in_specs=[anywhere] * 4,
        out_specs=[anywhere] * 4,
        scratch_shapes=[dma((2 + 2 * PIECES,))],
        compiler_params=pltpu.CompilerParams(vmem_limit_bytes=4 * 2**20),
        name="hand_over",
    )(*results)


def solution(mesh):
    ntp, nreq = mesh.shape["tp"], mesh.shape["req"]
    return jax.shard_map(
        lambda *arguments: per_device(ntp, nreq, *arguments),
        mesh=mesh,
        in_specs=(
            P("req", "tp", None, None),
            P("tp"),
            P("tp"),
            P("tp"),
            P("tp", None),
            P(("req", "tp"), None, None),
            P("req", None, "tp"),
            P("req", None, "tp"),
            P(),
            P(),
            P(),
            P(None, "req", "tp"),
            P(None, "req", "tp"),
            P(None, "req", "tp"),
            P(None, "req", None, None),
            P(None, "req", None),
            P(None, "req", None),
        ),
        out_specs=(
            P(None, "req", "tp"),
            P(None, "req", "tp"),
            P("req", "tp", None, None),
            P(("req", "tp"), None, None),
        ),
        check_vma=False,
    )
```

```python
import math

import jax
import jax.numpy as jnp
from jax import lax
from jax.experimental import pallas as pl
from jax.experimental.pallas import tpu as pltpu
from jax.sharding import PartitionSpec as P

MESH = pl.DeviceIdType.MESH
HIGH = lax.Precision.HIGHEST
F32 = jnp.float32
BF16 = jnp.bfloat16
I32 = jnp.int32

P_SIZE = 64
N = 128
G = 8
QH = 64
KVH = 8
HD = 128
PAGE = 16
STEPS = 2
ROWS = 4
PGS = 4
MV = 2
HPD = 8
HMV = 4
HEADS_PER_GROUP = 16
GROUP_CHANNELS = 1024
KVW = 2048
SLOTS = ROWS * PGS
SI = STEPS * ROWS
CH = HPD * P_SIZE
NEG = -1e30
EPSILON = 1e-05

T_AR, T_AL, T_HEAD, T_BR, T_BL, T_ROW = 0, 4, 8, 16, 18, 20
T_OWNPG, T_RECVPG, T_ISOWN, T_INV, T_GROUP, T_LEN, T_PAR = 24, 40, 56, 60, 76, 84, 88
T_RR, T_RL, T_REC = 96, 98, 100
PIECES = 4
REC, REC_X, REC_GATE, REC_MAPS, REC_RAW = 16, 0, 2, 4, 12


def dot_nt(a, b, precision=None):
    return lax.dot_general(
        a, b, (((1,), (1,)), ((), ())), precision=precision, preferred_element_type=F32
    )


def choose(source, base, count, block, most):
    picks = [jnp.int32(0)] * most
    seen = jnp.int32(0)
    for i in range(count):
        v = source[base + i]
        hit = v // count == block
        for k in range(most):
            picks[k] = jnp.where(hit & (seen == k), v - block * count, picks[k])
        seen = seen + hit.astype(I32)
    return picks


def choose_slots(source, base, count, block, most):
    picks = [jnp.int32(0)] * most
    seen = jnp.int32(0)
    for i in range(count):
        hit = source[base + i] // count == block
        for k in range(most):
            picks[k] = jnp.where(hit & (seen == k), i, picks[k])
        seen = seen + hit.astype(I32)
    return picks


def kernel(ntp, nreq, *refs):
    (
        state_hbm, gain_hbm, pool_hbm, x_hbm, gate_hbm, maps_hbm, q_hbm, entry_hbm,
        raw_hbm, rate_h, bias_h, skip_h, old_h, new_h, rsrc_h, hsrc_h, ctx_h,
        mixer_v, attn_v, fin_state, fin_pool,
        own, a_send, a_recv, rowbuf, b_send, b_recv, pool_v, c_send, c_recv, newp,
        gain_in, x_in, gate_in, maps_in, q_in, entry_in,
        p_own, p_recv, p_gain, p_scal, slot_scal, dt_v, decay_v, raw_t,
        xf, rec, r_send, r_recv, recf, xpad, x_t, qf, ef, maps_g, c_rows, outer, member, skip_row, gain_row,
        stash, ybuf, vis, x_send, l_send, x_pair, l_pair, xc_send, xc_recv, lc_send, lc_recv, lses_v, s_send, s_recv, m_send, m_recv, m_all,
        raw_in,
        rate_s, bias_s, skip_s, old_s, new_s, rsrc, hsrc, ctx, tab,
        in_sem, scalar_sem, r_ss, r_rs, m_ss, m_rs, a_ss, a_rs, p_ss, p_rs, b_ss, b_rs, c_ss, c_rs, pair_ss, pair_rs, x_ss, x_rs, l_ss, l_rs, s_ss, s_rs,
    ) = refs
    share = QH // ntp
    xrows = share * SI
    t = lax.axis_index("tp")
    r = lax.axis_index("req")
    t_right, t_left = lax.rem(t + 1, ntp), lax.rem(t + ntp - 1, ntp)
    r_right, r_left = lax.rem(r + 1, nreq), lax.rem(r + nreq - 1, nreq)
    dev = {"tr": (r, t_right), "tl": (r, t_left), "rr": (r_right, t), "rl": (r_left, t)}

    scalars = [
        pltpu.make_async_copy(src, dst, scalar_sem.at[k])
        for k, (src, dst) in enumerate(
            (
                (hsrc_h, hsrc), (rsrc_h, rsrc), (old_h, old_s), (ctx_h, ctx), (new_h, new_s),
                (rate_h, rate_s), (bias_h, bias_s), (skip_h, skip_s),
            )
        )
    ]
    loads = [
        pltpu.make_async_copy(state_hbm, own.at[:, pl.ds(0, HPD)], in_sem.at[0]),
        pltpu.make_async_copy(pool_hbm, pool_v, in_sem.at[1]),
        pltpu.make_async_copy(gain_hbm, gain_in, in_sem.at[2]),
        pltpu.make_async_copy(x_hbm, x_in, in_sem.at[3]),
        pltpu.make_async_copy(gate_hbm, gate_in, in_sem.at[4]),
        pltpu.make_async_copy(maps_hbm, maps_in, in_sem.at[5]),
        pltpu.make_async_copy(q_hbm, q_in, in_sem.at[6]),
        pltpu.make_async_copy(entry_hbm, entry_in, in_sem.at[7]),
        pltpu.make_async_copy(raw_hbm, raw_in, in_sem.at[8]),
    ]
    for c in scalars[:1] + loads[:1]:
        c.start()

    barrier = pltpu.get_barrier_semaphore()
    for name in ("rr", "rl"):
        pl.semaphore_signal(barrier, inc=1, device_id=dev[name], device_id_type=MESH)

    def peer(k):
        core, y_hi = (t + k) % 2, (t // 2 + k // 2) % 2
        return (t // 4 + k // 4) % (ntp // 4) * 4 + y_hi * 2 + core

    def each_peer(act):
        def far(n, _):
            act(n // 2 * 4 + 2 + n % 2)
            return 0

        def near(n, _):
            act(n // 2 * 4 + n % 2)
            return 0

        lax.fori_loop(0, ntp // 2, far, 0)
        lax.fori_loop(1, ntp // 2, near, 0)

    def greet(k):
        pl.semaphore_signal(barrier, inc=1, device_id=(r, peer(k)), device_id_type=MESH)

    each_peer(greet)

    for c in scalars[1:] + loads[1:]:
        c.start()

    with jax.named_scope("scalars"):
        scalars[0].wait()
    for k, v in enumerate(choose(hsrc, t_right * HPD, HPD, t, HMV)):
        tab[T_AR + k] = v
    for k, v in enumerate(choose(hsrc, t_left * HPD, HPD, t, HMV)):
        tab[T_AL + k] = v

    loads[0].wait()

    def pack_a(n, _):
        d, k, q = n // (HMV * ROWS), (n // ROWS) % HMV, n % ROWS
        a_send[d, k, q] = own[q, tab[T_AR + d * HMV + k]].astype(BF16)
        return 0

    lax.fori_loop(0, 2 * HMV * ROWS, pack_a, 0)

    with jax.named_scope("entry_barrier"):
        pl.semaphore_wait(barrier, ntp + 1)

    def send(src, dst, ss, rs, to):
        return pltpu.make_async_remote_copy(
            src_ref=src, dst_ref=dst, send_sem=ss, recv_sem=rs, device_id=to, device_id_type=MESH
        )

    run = 4
    long_way = (lax.rem(r, run) == run - 1, lax.rem(r, run) == 0)

    def start_long(copies):
        for c, far in zip(copies, long_way):
            pl.when(far)(c.start)

    def start_short(copies):
        for c, far in zip(copies, long_way):
            pl.when(jnp.logical_not(far))(c.start)

    a_cp = [
        send(a_send.at[d], a_recv.at[d], a_ss.at[d], a_rs.at[d], dev[("tr", "tl")[d]])
        for d in range(2)
    ]
    for c in a_cp:
        c.start()

    for c in scalars[1:]:
        c.wait()
    loads[2].wait()
    sub = lax.broadcasted_iota(I32, (HPD, N), 0)
    lane = lax.broadcasted_iota(I32, (HPD, N), 1)
    p_own[0:HPD, 0:P_SIZE] = gain_in[...]
    wide = p_own[0:HPD, :]
    p_own[0:HPD, :] = jnp.where(lane < P_SIZE, wide, pltpu.roll(wide, P_SIZE, 1))
    scal = jnp.zeros((HPD, N), F32)
    for h in range(HPD):
        for place, ref in enumerate((bias_s, rate_s, skip_s)):
            scal = jnp.where((sub == h) & (lane == place), ref[h], scal)
    p_own[HPD : 2 * HPD, :] = scal
    p_cp = [
        send(p_own, p_recv.at[d], p_ss.at[d], p_rs.at[d], dev[("tr", "tl")[d]]) for d in range(2)
    ]
    for c in p_cp:
        c.start()

    for k, v in enumerate(choose(rsrc, r_right * ROWS, ROWS, r, MV)):
        tab[T_BR + k] = v
    for k, v in enumerate(choose(rsrc, r_left * ROWS, ROWS, r, MV)):
        tab[T_BL + k] = v
    for k, v in enumerate(choose_slots(rsrc, r * ROWS, ROWS, r_right, MV)):
        tab[T_RR + k] = v
    for k, v in enumerate(choose_slots(rsrc, r * ROWS, ROWS, r_left, MV)):
        tab[T_RL + k] = v
    records = [jnp.int32(0)] * ROWS
    for block, base in ((r_left, ROWS), (r, 0), (r_right, ROWS + MV)):
        rank = jnp.int32(0)
        for i in range(ROWS):
            v = rsrc[block * ROWS + i]
            hit = v // ROWS == r
            where = jnp.clip(rank, 0, MV - 1) + base if base else i
            for q in range(ROWS):
                records[q] = jnp.where(hit & (v - r * ROWS == q), where, records[q])
            rank = rank + hit.astype(I32)
    for q in range(ROWS):
        tab[T_REC + q] = records[q]
    lefts, rights = jnp.int32(0), jnp.int32(0)
    for j in range(HPD):
        v = hsrc[t * HPD + j]
        far = v // HPD - t
        place = jnp.where(far == 0, v - t * HPD, jnp.where(far < 0, HPD + lefts, HPD + HMV + rights))
        tab[T_HEAD + j] = jnp.clip(place, 0, HPD + 2 * HMV - 1)
        tab[T_PAR + j] = jnp.clip(v - t * HPD + HPD, 0, 3 * HPD - 1)
        tab[T_GROUP + j] = v // HEADS_PER_GROUP
        lefts = lefts + (far < 0).astype(I32)
        rights = rights + (far > 0).astype(I32)
    lefts, rights = jnp.int32(0), jnp.int32(0)
    for i in range(ROWS):
        v = rsrc[r * ROWS + i]
        far = v // ROWS - r
        here = jnp.where(far == 0, v - r * ROWS, 0)
        away = jnp.where(far < 0, lefts, MV + rights)
        away = jnp.clip(jnp.where(far == 0, 0, away), 0, 2 * MV - 1)
        tab[T_ROW + i] = jnp.where(far == 0, here, ROWS + away)
        tab[T_ISOWN + i] = (far == 0).astype(I32)
        tab[T_LEN + i] = ctx[v]
        for g in range(PGS):
            tab[T_OWNPG + i * PGS + g] = old_s[here, 0, g]
            tab[T_RECVPG + i * PGS + g] = away * PGS + g
        lefts = lefts + (far < 0).astype(I32)
        rights = rights + (far > 0).astype(I32)

    for c in loads[3:6] + loads[8:9]:
        c.wait()
    xpad[...] = jnp.zeros_like(xpad)
    rec[...] = jnp.zeros_like(rec)
    for s in range(STEPS):
        xpad[s * ROWS : (s + 1) * ROWS, 0:HPD] = raw_in[s]
        xf[0, s * ROWS : (s + 1) * ROWS, :] = x_in[s].astype(F32)
        xf[1, s * ROWS : (s + 1) * ROWS, :] = gate_in[s].astype(F32)
    for i in range(ROWS):
        parts = [xf[0, k : k + 1, :] for k in (i, ROWS + i)]
        parts += [xf[1, k : k + 1, :] for k in (i, ROWS + i)]
        for s in range(STEPS):
            maps = maps_in[s, i].astype(F32)
            for bc in range(2):
                parts += [maps[bc : bc + 1, h * CH : (h + 1) * CH] for h in range(2)]
        raws = jnp.concatenate([xpad[i : i + 1, 0:N], xpad[ROWS + i : ROWS + i + 1, 0:N]], axis=1)
        rest = jnp.concatenate([raws, jnp.zeros((1, CH - 2 * N), F32)], axis=1)
        for _ in range(3):
            top = rest.astype(BF16).astype(F32)
            parts.append(top)
            rest = rest - top
        parts.append(rest)
        rec[i] = jnp.concatenate(parts, axis=0).astype(BF16)
    for d in range(2):
        for k in range(MV):
            r_send[d, k] = rec[tab[T_RR + d * MV + k]]

    r_cp = [
        send(r_send.at[d], r_recv.at[d], r_ss.at[d], r_rs.at[d], dev[("rr", "rl")[d]])
        for d in range(2)
    ]
    for c in r_cp:
        c.start()

    loads[1].wait()

    def pack_c(n, _):
        d, k, g = n // (MV * PGS), (n // PGS) % MV, n % PGS
        c_send[n] = pool_v[old_s[tab[T_BR + d * MV + k], 0, g]]
        return 0

    lax.fori_loop(0, 2 * MV * PGS, pack_c, 0)

    c_cp = []
    for d in range(2):
        part = pl.ds(d * MV * PGS, MV * PGS)
        c_cp.append(
            send(c_send.at[part], c_recv.at[part], c_ss.at[d], c_rs.at[d], dev[("rr", "rl")[d]])
        )
    start_long(c_cp)

    for i in range(SLOTS):
        found = jnp.int32(0)
        for e in range(SLOTS):
            found = jnp.where(new_s[e // PGS, 0, e % PGS] == i, e, found)
        tab[T_INV + i] = found
    for c in loads[6:8]:
        c.wait()
    for s in range(STEPS):
        part = slice(s * ROWS, (s + 1) * ROWS)
        qf[part, :] = q_in[s].astype(F32)
        ef[part, :] = entry_in[s].astype(F32)

    rowid = lax.broadcasted_iota(I32, (QH, ROWS * PGS * PAGE), 0)
    colid = lax.broadcasted_iota(I32, (QH, ROWS * PGS * PAGE), 1)
    row_i = rowid % ROWS
    limit = (rowid // ROWS) % STEPS
    for i in range(ROWS):
        limit = limit + jnp.where(row_i == i, tab[T_LEN + i], 0)
    place = ((colid // PAGE) % PGS * ntp + t) * PAGE + colid % PAGE
    seen = (row_i == colid // (PGS * PAGE)) & (place <= limit)
    vis[...] = jnp.where(seen, 1.0, 0.0)

    with jax.named_scope("params_arrive"):
        for c in p_cp + r_cp:
            c.wait_recv()
    start_short(c_cp)
    for part, buf in enumerate((p_gain, p_scal)):
        rows = slice(part * HPD, (part + 1) * HPD)
        buf[0:HPD, :] = p_recv[0, rows, :]
        buf[HPD : 2 * HPD, :] = p_own[rows, :]
        buf[2 * HPD : 3 * HPD, :] = p_recv[1, rows, :]
    for j in range(HPD):
        slot_scal[j : j + 1, :] = p_scal[pl.ds(tab[T_PAR + j], 1), :]
    bias, rate, skip = (slot_scal[:, k : k + 1] for k in range(3))
    for q in range(ROWS):
        at = tab[T_REC + q]
        mine = rec[jnp.minimum(at, ROWS - 1)].astype(F32)
        away = jnp.maximum(at - ROWS, 0)
        came = r_recv[away // MV, away % MV].astype(F32)
        recf[q] = jnp.where(at < ROWS, mine, came)
    for q in range(ROWS):
        raws = recf[q, REC_RAW : REC_RAW + 1, :]
        for k in range(1, 3):
            raws = raws + recf[q, REC_RAW + k : REC_RAW + k + 1, :]
        for s in range(STEPS):
            k = s * ROWS + q
            xf[0, k : k + 1, :] = recf[q, REC_X + s : REC_X + s + 1, :]
            xf[1, k : k + 1, :] = recf[q, REC_GATE + s : REC_GATE + s + 1, :]
            xpad[k : k + 1, 0:N] = raws[:, s * N : (s + 1) * N]
            for bc in range(2):
                for g in range(G):
                    row = REC_MAPS + (s * 2 + bc) * 2 + g // (G // 2)
                    lanes = slice(g % (G // 2) * N, (g % (G // 2) + 1) * N)
                    maps_g[g, 2 * k + bc : 2 * k + bc + 1, :] = recf[q, row : row + 1, lanes]
    raw_t[...] = xpad[:, 0:N].T[0:HPD, :]
    xpad[0:SI, :] = xf[0]
    for m in range(CH // N):
        x_t[m * N : (m + 1) * N, :] = xpad[:, m * N : (m + 1) * N].T
    v = raw_t[...] + bias
    dt = jnp.maximum(v, 0.0) + jnp.log1p(jnp.exp(-jnp.abs(v)))
    dt_v[...] = dt
    decay_v[...] = jnp.exp(-rate * dt)
    lane1 = lax.broadcasted_iota(I32, (1, N), 1)
    for m in range(CH // N):
        lanes = slice(m * N, (m + 1) * N)
        first = p_gain[pl.ds(tab[T_PAR + 2 * m], 1), :]
        second = p_gain[pl.ds(tab[T_PAR + 2 * m + 1], 1), :]
        gain_row[:, lanes] = jnp.where(lane1 < P_SIZE, first, second)
        skip_row[:, lanes] = jnp.where(
            lane1 < P_SIZE,
            jnp.broadcast_to(skip[2 * m : 2 * m + 1], (1, N)),
            jnp.broadcast_to(skip[2 * m + 1 : 2 * m + 2], (1, N)),
        )
    lane64 = lax.broadcasted_iota(I32, (P_SIZE, N), 1)

    def prepare(j, _):
        group = tab[T_GROUP + j]
        member[pl.ds(pl.multiple_of(j * P_SIZE, P_SIZE), P_SIZE), :] = jnp.where(
            lane64 % G == group, 1.0, 0.0
        )
        both = maps_g[group]
        dts = dt_v[pl.ds(j, 1), :]
        cols = x_t[pl.ds(pl.multiple_of(j * P_SIZE, P_SIZE), P_SIZE), :]
        for k in range(SI):
            outer[k, j] = cols[:, k : k + 1] * (dts[:, k : k + 1] * both[2 * k : 2 * k + 1, :])
            c_rows[k, pl.ds(j, 1), :] = both[2 * k + 1 : 2 * k + 2, :]
        return 0

    lax.fori_loop(0, HPD, prepare, 0)

    with jax.named_scope("heads_arrive"):
        for c in a_cp:
            c.wait_recv()

    def take_a(n, _):
        k, q = n // ROWS, n % ROWS
        own[q, HPD + k] = a_recv[k // HMV, k % HMV, q].astype(F32)
        return 0

    lax.fori_loop(0, 2 * HMV * ROWS, take_a, 0)

    diagonal = lax.broadcasted_iota(I32, (HPD, CH), 0) == (
        lax.broadcasted_iota(I32, (HPD, CH), 1) // P_SIZE
    )
    for i in range(ROWS):

        def step(j, _):
            now = own[i, tab[T_HEAD + j]]
            fade = decay_v[pl.ds(j, 1), :]
            for s in range(STEPS):
                k = s * ROWS + i
                now = fade[:, k : k + 1] * now + outer[k, j]
                stash[s, pl.ds(pl.multiple_of(j * P_SIZE, P_SIZE), P_SIZE), :] = now
            rowbuf[i, j] = now
            return 0

        lax.fori_loop(0, HPD, step, 0)
        for s in range(STEPS):
            k = s * ROWS + i
            now = stash[s]
            top = now.astype(BF16)
            low = (now - top.astype(F32)).astype(BF16)
            c8 = c_rows[k].astype(BF16)
            y = dot_nt(c8, top) + dot_nt(c8, low)
            ybuf[k : k + 1, :] = jnp.sum(jnp.where(diagonal, y, 0.0), axis=0, keepdims=True)

    gate = xf[1]
    gated = (ybuf[...] + skip_row[...] * xf[0]) * (gate / (1.0 + jnp.exp(-gate)))
    packed = sub == lane // G
    squares = jnp.dot(gated * gated, member[...], precision=HIGH, preferred_element_type=F32)
    s_send[...] = jnp.sum(jnp.where(packed, squares, 0.0), axis=0, keepdims=True)

    def s_copy(k):
        return send(s_send, s_recv.at[k], s_ss.at[k], s_rs.at[k], (r, peer(k)))

    each_peer(lambda k: s_copy(k).start())
    s_recv[0] = s_send[...]

    def pack_b(n, _):
        d, k, j = n // (MV * HPD), (n // HPD) % MV, n % HPD
        b_send[d, k, j] = rowbuf[tab[T_BR + d * MV + k], j].astype(BF16)
        return 0

    lax.fori_loop(0, 2 * MV * HPD, pack_b, 0)
    b_cp = [
        send(b_send.at[d], b_recv.at[d], b_ss.at[d], b_rs.at[d], dev[("rr", "rl")[d]])
        for d in range(2)
    ]

    start_long(b_cp)

    with jax.named_scope("pages_arrive"):
        for c in c_cp:
            c.wait_recv()

    offset = lax.broadcasted_iota(I32, (PAGE, KVW), 0)

    def take_page(n, _):
        i, g = n // PGS, n % PGS
        mine = pool_v[tab[T_OWNPG + n]].astype(F32)
        came = c_recv[tab[T_RECVPG + n]].astype(F32)
        page = jnp.where(tab[T_ISOWN + i] == 1, mine, came)
        for s in range(STEPS):
            position = tab[T_LEN + i] + s
            logical = position // PAGE
            hit = (logical % ntp == t) & (logical // ntp == g)
            at = jnp.where(hit, position % PAGE, -1)
            page = jnp.where(offset == at, ef[pl.ds(s * ROWS + i, 1), :], page)
        newp[n] = page.astype(BF16)
        return 0

    lax.fori_loop(0, SLOTS, take_page, 0)

    eye = lax.broadcasted_iota(I32, (xrows, N), 0) == lax.broadcasted_iota(I32, (xrows, N), 1)
    shown = vis[...] > 0.5
    per = QH // KVH
    for g in range(KVH):
        q = jnp.concatenate(
            [qf[:, (g * per + h) * HD : (g * per + h + 1) * HD] for h in range(per)], axis=0
        ).astype(BF16)
        keys = newp[:, :, g * HD : (g + 1) * HD].reshape(SLOTS * PAGE, HD)
        values = newp[:, :, (KVH + g) * HD : (KVH + g + 1) * HD].reshape(SLOTS * PAGE, HD)
        scores = jnp.where(shown, dot_nt(q, keys) * (1.0 / math.sqrt(HD)), NEG)
        peak = jnp.max(scores, axis=1, keepdims=True)
        weights = jnp.where(shown, jnp.exp(scores - peak), 0.0).astype(BF16)
        total = jnp.sum(weights.astype(F32), axis=1, keepdims=True)
        part = jnp.dot(weights, values, preferred_element_type=F32)
        safe = jnp.maximum(total, 1e-30)
        part = (part / safe).astype(BF16)
        lse = jnp.where(total > 0.0, peak + jnp.log(safe), NEG)
        for e in range(per // share):
            rows = slice(e * xrows, (e + 1) * xrows)
            dest = g * (per // share) + e
            x_send[dest % 2, dest // 2] = part[rows]
            l_send[dest % 2, dest // 2] = jnp.sum(
                jnp.where(eye, lse[rows], 0.0), axis=0, keepdims=True
            )

    side = t % 2
    other = (r, t + 1 - 2 * side)
    pair_cp = [
        send(x_send.at[1 - side], x_pair, pair_ss.at[0], pair_rs.at[0], other),
        send(l_send.at[1 - side], l_pair, pair_ss.at[1], pair_rs.at[1], other),
    ]
    for c in pair_cp:
        c.start()

    with jax.named_scope("squares_arrive"):
        each_peer(lambda k: s_copy(k).wait_recv())
    squares = jnp.sum(s_recv[...], axis=0)
    scale = jnp.where(packed, lax.rsqrt(squares * (1.0 / GROUP_CHANNELS) + EPSILON), 0.0)
    mixed = gated * dot_nt(scale, member[...], HIGH) * gain_row[...]
    for q in range(ROWS):
        for s in range(STEPS):
            for m in range(CH // N):
                k = s * ROWS + q
                m_all[q, s * (CH // N) + m : s * (CH // N) + m + 1, :] = mixed[
                    k : k + 1, m * N : (m + 1) * N
                ]
    for d in range(2):
        for k in range(MV):
            m_send[d, k] = m_all[tab[T_BR + d * MV + k]]
    m_cp = [
        send(m_send.at[d], m_recv.at[d], m_ss.at[d], m_rs.at[d], dev[("rr", "rl")[d]])
        for d in range(2)
    ]
    for c in m_cp:
        c.start()

    start_short(b_cp)
    with jax.named_scope("pair_arrives"):
        for c in pair_cp:
            c.wait_recv()
    chips = ntp // 2
    mine, came = l_send[side].reshape(chips, N), l_pair[...].reshape(chips, N)
    peak = jnp.maximum(mine, came)
    w_mine, w_came = jnp.exp(mine - peak), jnp.exp(came - peak)
    total = w_mine + w_came
    lses_v[...] = peak + jnp.log(total)
    xpad[0:chips, 0:N] = w_mine / total
    xpad[chips : 2 * chips, 0:N] = w_came / total
    cols = xpad[:, 0:N].T
    for k in range(chips):
        both = cols[0:xrows, k : k + 1] * x_send[side, k].astype(F32)
        both = both + cols[0:xrows, chips + k : chips + k + 1] * x_pair[k].astype(F32)
        xc_send[k] = both.astype(BF16)
        lc_send[k] = lses_v[k : k + 1, :]

    def x_copies(k):
        to = peer(2 * k)
        return (
            send(xc_send.at[to // 2], xc_recv.at[k], x_ss.at[k], x_rs.at[k], (r, to)),
            send(lc_send.at[to // 2], lc_recv.at[k], l_ss.at[k], l_rs.at[k], (r, to)),
        )

    def each_chip(act):
        def one(k, _):
            for c in x_copies(k):
                act(c)
            return 0

        lax.fori_loop(1, chips, one, 0)

    each_chip(lambda c: c.start())
    xc_recv[0] = xc_send[t // 2]
    lc_recv[0] = lc_send[t // 2]

    def place_page(n, _):
        fin_pool[n] = newp[tab[T_INV + n]]
        return 0

    lax.fori_loop(0, SLOTS, place_page, 0)

    with jax.named_scope("partials_arrive"):
        each_chip(lambda c: c.wait_recv())
    lses = lc_recv[...].reshape(chips, N)
    w = jnp.exp(lses - jnp.max(lses, axis=0, keepdims=True))
    w = w / jnp.sum(w, axis=0, keepdims=True)
    xpad[0:chips, 0:N] = w
    cols = xpad[:, 0:N].T
    total = jnp.zeros((xrows, HD), F32)
    for k in range(chips):
        total = total + cols[0:xrows, k : k + 1] * xc_recv[k].astype(F32)
    for s in range(STEPS):
        for h in range(share):
            attn_v[s, :, h * HD : (h + 1) * HD] = total[
                h * SI + s * ROWS : h * SI + (s + 1) * ROWS
            ].astype(BF16)

    for c in m_cp:
        c.wait_recv()
    for d in range(2):
        for k in range(MV):
            m_all[ROWS + d * MV + k] = m_recv[d, k]
    for i in range(ROWS):
        row = m_all[tab[T_ROW + i]]
        for s in range(STEPS):
            for m in range(CH // N):
                ybuf[s * ROWS + i : s * ROWS + i + 1, m * N : (m + 1) * N] = row[
                    s * (CH // N) + m : s * (CH // N) + m + 1
                ]
    for s in range(STEPS):
        mixer_v[s] = ybuf[s * ROWS : (s + 1) * ROWS].astype(BF16)

    with jax.named_scope("rows_arrive"):
        for c in b_cp:
            c.wait_recv()

    def place_row(n, _):
        i, j = n // HPD, n % HPD
        at = tab[T_ROW + i]
        away = jnp.maximum(at - ROWS, 0)
        mine = rowbuf[jnp.minimum(at, ROWS - 1), j]
        came = b_recv[away // MV, away % MV, j].astype(F32)
        fin_state[i, j] = jnp.where(at < ROWS, mine, came)
        return 0

    lax.fori_loop(0, ROWS * HPD, place_row, 0)

    with jax.named_scope("all_sent"):
        for c in a_cp + p_cp + r_cp + c_cp + b_cp + m_cp + pair_cp:
            c.wait_send()
        each_peer(lambda k: s_copy(k).wait_send())
        each_chip(lambda c: c.wait_send())


def hand_over(mixer, attn, state, pool, mixer_out, attn_out, state_out, pool_out, sem):
    pieces = [(mixer, mixer_out), (attn, attn_out)]
    for src, dst in ((state, state_out), (pool, pool_out)):
        size = src.shape[0] // PIECES
        for k in range(PIECES):
            part = pl.ds(k * size, size)
            pieces.append((src.at[part], dst.at[part]))
    copies = [pltpu.make_async_copy(a, b, sem.at[k]) for k, (a, b) in enumerate(pieces)]
    for c in copies:
        c.start()
    for c in copies:
        c.wait()


def per_device(ntp, nreq, *arguments):
    (
        scan_state, decay_rate, step_bias, skip_gain, norm_gain, page_pool, old_table, new_table,
        request_source, head_source, context_lengths, mixer_input, mixer_gate, step_raw, state_maps,
        queries, new_entries,
    ) = arguments
    xrows = QH // ntp * SI
    anywhere = pl.BlockSpec(memory_space=pl.ANY)
    dma = pltpu.SemaphoreType.DMA
    scratch = [
        ((ROWS, HPD + 2 * HMV, P_SIZE, N), F32),
        ((2, HMV, ROWS, P_SIZE, N), BF16),
        ((2, HMV, ROWS, P_SIZE, N), BF16),
        ((ROWS, HPD, P_SIZE, N), F32),
        ((2, MV, HPD, P_SIZE, N), BF16),
        ((2, MV, HPD, P_SIZE, N), BF16),
        ((SLOTS, PAGE, KVW), BF16),
        ((2 * MV * PGS, PAGE, KVW), BF16),
        ((2 * MV * PGS, PAGE, KVW), BF16),
        ((SLOTS, PAGE, KVW), BF16),
        (norm_gain.shape, F32),
        (mixer_input.shape, BF16),
        (mixer_gate.shape, BF16),
        (state_maps.shape, BF16),
        (queries.shape, BF16),
        (new_entries.shape, BF16),
        ((2 * HPD, N), F32),
        ((2, 2 * HPD, N), F32),
        ((3 * HPD, N), F32),
        ((3 * HPD, N), F32),
        ((HPD, N), F32),
        ((HPD, N), F32),
        ((HPD, N), F32),
        ((HPD, N), F32),
        ((2, SI, CH), F32),
        ((ROWS, REC, CH), BF16),
        ((2, MV, REC, CH), BF16),
        ((2, MV, REC, CH), BF16),
        ((ROWS, REC, CH), F32),
        ((N, CH), F32),
        ((CH, N), F32),
        ((SI, QH * HD), F32),
        ((SI, KVW), F32),
        ((G, 2 * SI, N), F32),
        ((SI, HPD, N), F32),
        ((SI, HPD, P_SIZE, N), F32),
        ((CH, N), F32),
        ((1, CH), F32),
        ((1, CH), F32),
        ((STEPS, CH, N), F32),
        ((SI, CH), F32),
        ((QH, SLOTS * PAGE), F32),
        ((2, ntp // 2, xrows, HD), BF16),
        ((2, ntp // 2, 1, N), F32),
        ((ntp // 2, xrows, HD), BF16),
        ((ntp // 2, 1, N), F32),
        ((ntp // 2, xrows, HD), BF16),
        ((ntp // 2, xrows, HD), BF16),
        ((ntp // 2, 1, N), F32),
        ((ntp // 2, 1, N), F32),
        ((ntp // 2, N), F32),
        ((1, N), F32),
        ((ntp, 1, N), F32),
        ((2, MV, SI, N), F32),
        ((2, MV, SI, N), F32),
        ((ROWS + 2 * MV, SI, N), F32),
        (step_raw.shape, F32),
    ]
    results = pl.pallas_call(
        lambda *refs: kernel(ntp, nreq, *refs),
        out_shape=(
            pltpu.VMEM((STEPS, ROWS, CH), BF16),
            pltpu.VMEM((STEPS, ROWS, CH), BF16),
            pltpu.VMEM(scan_state.shape, F32),
            pltpu.VMEM(page_pool.shape, BF16),
        ),
        in_specs=[pl.BlockSpec(memory_space=pltpu.HBM)] * 17,
        out_specs=(pl.BlockSpec(memory_space=pltpu.VMEM),) * 4,
        scratch_shapes=[pltpu.VMEM(shape, dtype) for shape, dtype in scratch]
        + [
            *[pltpu.SMEM((HPD,), F32) for _ in range(3)],
            *[pltpu.SMEM((ROWS, 1, PGS), I32) for _ in range(2)],
            *[pltpu.SMEM(ints.shape, I32) for ints in (request_source, head_source, context_lengths)],
            pltpu.SMEM((128,), I32),
            dma((9,)),
            dma((8,)),
            *[dma((2,)) for _ in range(14)],
            *[dma((ntp,)) for _ in range(6)],
        ],
        compiler_params=pltpu.CompilerParams(
            collective_id=0, has_side_effects=True, vmem_limit_bytes=60 * 2**20
        ),
        name="decode",
    )(
        scan_state, norm_gain, page_pool, mixer_input, mixer_gate, state_maps, queries, new_entries,
        step_raw, decay_rate, step_bias, skip_gain, old_table.transpose(0, 2, 1), new_table.transpose(0, 2, 1),
        request_source, head_source, context_lengths,
    )
    return pl.pallas_call(
        hand_over,
        out_shape=[jax.ShapeDtypeStruct(x.shape, x.dtype) for x in results],
        in_specs=[anywhere] * 4,
        out_specs=[anywhere] * 4,
        scratch_shapes=[dma((2 + 2 * PIECES,))],
        compiler_params=pltpu.CompilerParams(vmem_limit_bytes=4 * 2**20),
        name="hand_over",
    )(*results)


def solution(mesh):
    ntp, nreq = mesh.shape["tp"], mesh.shape["req"]
    return jax.shard_map(
        lambda *arguments: per_device(ntp, nreq, *arguments),
        mesh=mesh,
        in_specs=(
            P("req", "tp", None, None),
            P("tp"),
            P("tp"),
            P("tp"),
            P("tp", None),
            P(("req", "tp"), None, None),
            P("req", None, "tp"),
            P("req", None, "tp"),
            P(),
            P(),
            P(),
            P(None, "req", "tp"),
            P(None, "req", "tp"),
            P(None, "req", "tp"),
            P(None, "req", None, None),
            P(None, "req", None),
            P(None, "req", None),
        ),
        out_specs=(
            P(None, "req", "tp"),
            P(None, "req", "tp"),
            P("req", "tp", None, None),
            P(("req", "tp"), None, None),
        ),
        check_vma=False,
    )
```
